512 devices in a mesh: ens: 2 (over x_hi), lat: 32 (over x_lo, y, core), lon: 8 (over z).
Axes of the slice: x: 4 (x_hi: 2, x_lo: 2; x = x_hi * 2 + x_lo), y: 8, z: 8, core: 2. Of those that a mesh axis runs over, the one named last changes fastest.
Arguments:
- fields: bfloat16 [2, 128, 1440, 128], P('ens', 'lat', 'lon'), may hold values from -6 to 6
- cotangent: bfloat16 [2, 128, 1440, 128], P('ens', 'lat', 'lon'), may hold values from -6 to 6
- basis_weights: bfloat16 [3, 128, 12], P(None, 'lat'), may hold values from -1.75 to 1.75
- band_support: int32 [32, 3], P('lat'), may hold values from 0 to 1, as said below
- spectrum_real: float32 [3, 128, 720], P(None, 'lat'), may hold values from -6 to 6
- spectrum_imag: float32 [3, 128, 720], P(None, 'lat'), may hold values from -6 to 6
- filter_weights: bfloat16 [3, 128, 128], replicated, may hold values from -0.3125 to 0.3125
- inner_weights: bfloat16 [128, 256], replicated, may hold values from -0.5 to 0.5
- outer_weights: bfloat16 [256, 128], replicated, may hold values from -0.375 to 0.375
Outputs:
- field_grad: bfloat16 [2, 128, 1440, 128], P('ens', 'lat', 'lon')
- filter_grad: float32 [3, 128, 128], replicated
- inner_grad: float32 [128, 256], replicated
- outer_grad: float32 [256, 128], replicated
The draws below stay inside these ranges and needn't reach their ends.
Inputs may be any that keep to these rules, and one draw needn't show every extreme that they name: `band_support`: the middle column is 1 in every band; the bands among the first and the last max(8, 1), and the bands 32 // 2 - 1, 16 and 17, have all three columns 1; band 32 // 4 has a 0 in its first column.
All inputs are finite; a program needn't handle non-finite values.
Results may differ from the reference program's by a relative error of at most 0.019.
Values may be sent and summed in bfloat16 or wider, within the bound.
No kernel may reach another device: no remote copies, remote signals or barrier semaphores. Data moves between devices by JAX's collectives and lax.ppermute only.
A program may use at most 64 MiB of HBM per device.

```python
import math
import jax
import jax.numpy as jnp
from jax import lax

C = 128
HID = 256
NLON = 1440
BASIS = 3
LAT_DEV = 4
MODES = 720
NLAT = 128
NBANDS = 32
ENS = 2


def draw_band_support(key, part):
    key = jax.random.fold_in(key, 11)
    band_ids = jnp.arange(NBANDS, dtype=jnp.int32)
    border = max(NBANDS // 4, 1)
    centre = NBANDS // 2
    polar_band = (band_ids < border) | (band_ids >= NBANDS - border)
    central_band = (band_ids >= centre - 1) & (band_ids <= centre + 1)
    full_band = polar_band | central_band
    tosses = jax.random.randint(key, (NBANDS, 2), 0, 2, dtype=jnp.int32)
    flanks = jnp.where(full_band[:, None], 1, tosses)
    flanks = flanks.at[NBANDS // 4, 0].set(0)
    middle = jnp.ones((NBANDS,), jnp.int32)
    return jnp.stack([flanks[:, 0], middle, flanks[:, 1]], axis=1).astype(jnp.int32)


def block_levels(stream_key, dims, split, least, top_value):
    level = 1.0
    for dim, shards_of in split:
        heights = jax.random.uniform(jax.random.fold_in(jax.random.fold_in(stream_key, 6), dim), (shards_of,), jnp.float32, least / len(split), top_value / len(split))
        level = level * jnp.repeat(jnp.exp(heights), dims[dim] // shards_of).reshape((-1,) + (1,) * (len(dims) - 1 - dim))
    return level


def gaussian(stream_key, extent, deviation, limit, split=(), held_as=jnp.bfloat16):
    entries = jax.random.normal(stream_key, extent, jnp.float32) * deviation
    if len(split) > 0:
        entries = block_levels(stream_key, extent, split, -0.22, 0.18) * entries
    return jnp.clip(entries, min=-limit, max=limit).astype(held_as)


def setup_inputs(seed: int = 0) -> dict:
    keys = jax.random.split(jax.random.key(seed), 10)
    fields = gaussian(keys[0], (ENS, NLAT, NLON, C), 1.0, 6.0, ((0, 2), (1, 32), (2, 8)))
    cotangent = gaussian(keys[1], (ENS, NLAT, NLON, C), 1.0, 6.0, ((0, 2), (1, 32), (2, 8)))
    basis_weights = gaussian(keys[2], (BASIS, NLAT, 3 * LAT_DEV), (3 * LAT_DEV) ** -0.5, 1.75, ((1, 32),))
    band_support = draw_band_support(jax.random.fold_in(keys[9], 71), 0)
    spectrum_real = gaussian(keys[4], (BASIS, NLAT, MODES), 1.0, 6.0, ((1, 32),), jnp.float32)
    spectrum_imag = gaussian(keys[5], (BASIS, NLAT, MODES), 1.0, 6.0, ((1, 32),), jnp.float32)
    filter_weights = gaussian(keys[6], (BASIS, C, C), (BASIS * C) ** -0.5, 0.3125)
    inner_weights = gaussian(keys[7], (C, HID), C ** -0.5, 0.5)
    outer_weights = gaussian(keys[8], (HID, C), HID ** -0.5, 0.375)
    return {"fields": fields, "cotangent": cotangent, "basis_weights": basis_weights, "band_support": band_support, "spectrum_real": spectrum_real, "spectrum_imag": spectrum_imag, "filter_weights": filter_weights, "inner_weights": inner_weights, "outer_weights": outer_weights}


GELU_SCALE = 0.7978845608028654
CUBIC_TERM = 0.044715

def gelu_parts(hidden):
    inner_part = GELU_SCALE * (hidden + CUBIC_TERM * hidden * hidden * hidden)
    tangent = jnp.tanh(inner_part)
    gelu_value = 0.5 * hidden * (1.0 + tangent)
    gelu_slope = 0.5 * (1.0 + tangent) + 0.5 * hidden * (1.0 - tangent * tangent) * GELU_SCALE * (1.0 + 3.0 * CUBIC_TERM * hidden * hidden)
    return (gelu_value, gelu_slope)

def dft_tables(length, mode_count):
    column = jnp.arange(length, dtype=jnp.int32)
    frequency = jnp.arange(mode_count, dtype=jnp.int32)
    phase_angle = (column[:, None] * frequency[None, :] % length).astype(jnp.float32) * (2.0 * math.pi / length)
    forward_cos = jnp.cos(phase_angle).astype(jnp.bfloat16)
    forward_sin = (-jnp.sin(phase_angle)).astype(jnp.bfloat16)
    weight = jnp.where(frequency == 0, 1.0, 2.0).astype(jnp.float32) / length
    inverse_cos = (weight[:, None] * jnp.cos(phase_angle.T)).astype(jnp.bfloat16)
    inverse_sin = (-weight[:, None] * jnp.sin(phase_angle.T)).astype(jnp.bfloat16)
    return (forward_cos, forward_sin, inverse_cos, inverse_sin)

def filter_rows(basis_rows, spec_real, spec_imag, tables):
    forward_cos, forward_sin, inverse_cos, inverse_sin = [t.astype(jnp.float32) for t in tables]
    wide_basis = basis_rows.astype(jnp.float32)
    part_a = jnp.einsum('krcj,jm->krcm', wide_basis, forward_cos)
    part_b = jnp.einsum('krcj,jm->krcm', wide_basis, forward_sin)
    gain_a = spec_real[:, :, None, :]
    gain_b = spec_imag[:, :, None, :]
    filt_a = (gain_a * part_a - gain_b * part_b).astype(jnp.bfloat16).astype(jnp.float32)
    filt_b = (gain_a * part_b + gain_b * part_a).astype(jnp.bfloat16).astype(jnp.float32)
    result = jnp.einsum('krcm,mj->krcj', filt_a, inverse_cos) + jnp.einsum('krcm,mj->krcj', filt_b, inverse_sin)
    return result.astype(jnp.bfloat16)

def adjoint_rows(cot_rows, spec_real, spec_imag, tables):
    forward_cos, forward_sin, inverse_cos, inverse_sin = [t.astype(jnp.float32) for t in tables]
    wide_cot = cot_rows.astype(jnp.float32)
    grad_a = jnp.einsum('krcj,mj->krcm', wide_cot, inverse_cos)
    grad_b = jnp.einsum('krcj,mj->krcm', wide_cot, inverse_sin)
    gain_a = spec_real[:, :, None, :]
    gain_b = spec_imag[:, :, None, :]
    back_a = (gain_a * grad_a + gain_b * grad_b).astype(jnp.bfloat16).astype(jnp.float32)
    back_b = (gain_a * grad_b - gain_b * grad_a).astype(jnp.bfloat16).astype(jnp.float32)
    result = jnp.einsum('krcm,jm->krcj', back_a, forward_cos) + jnp.einsum('krcm,jm->krcj', back_b, forward_sin)
    return result.astype(jnp.bfloat16)

def dense_coupling(basis_weights, band_support):
    count = basis_weights.shape[0]
    total_rows = basis_weights.shape[1]
    band_rows = basis_weights.shape[2] // 3
    mask_rows = jnp.repeat(jnp.repeat(band_support, band_rows, axis=0), band_rows, axis=1).astype(jnp.float32)
    masked = basis_weights.astype(jnp.float32) * mask_rows[None]

    def place(row_weights, row_index):
        blank_row = jnp.zeros((count, total_rows + 2 * band_rows), jnp.float32)
        start_col = (row_index // band_rows * band_rows).astype(jnp.int32)
        return lax.dynamic_update_slice(blank_row, row_weights, (jnp.int32(0), start_col))
    row_ids = jnp.arange(total_rows, dtype=jnp.int32)
    placed = jax.vmap(place, in_axes=(1, 0), out_axes=1)(masked, row_ids)
    return placed[:, :, band_rows:band_rows + total_rows]

def reference(fields, cotangent, basis_weights, band_support, spectrum_real, spectrum_imag, filter_weights, inner_weights, outer_weights):
    tables = dft_tables(fields.shape[2], spectrum_real.shape[2])
    coupling = dense_coupling(basis_weights, band_support)
    grad_scale = 1.0 / math.sqrt(fields.shape[0] * fields.shape[1] * fields.shape[2])
    filter_w = filter_weights.astype(jnp.float32)
    inner_w = inner_weights.astype(jnp.float32)
    outer_w = outer_weights.astype(jnp.float32)
    field_grads = []
    filter_total = jnp.zeros(filter_weights.shape, jnp.float32)
    inner_total = jnp.zeros(inner_weights.shape, jnp.float32)
    outer_total = jnp.zeros(outer_weights.shape, jnp.float32)
    for member_id in range(fields.shape[0]):
        member = fields[member_id].astype(jnp.float32)
        member_cot = cotangent[member_id].astype(jnp.float32)
        basis_rows = jnp.einsum('kir,rjc->kicj', coupling, member).astype(jnp.bfloat16)
        filtered = filter_rows(basis_rows, spectrum_real, spectrum_imag, tables).astype(jnp.float32)
        mixed_out = jnp.einsum('kicj,kcd->ijd', filtered, filter_w)
        state_rows = (member + mixed_out).astype(jnp.bfloat16).astype(jnp.float32)
        hidden = jnp.einsum('ijc,ch->ijh', state_rows, inner_w)
        gelu_value, gelu_slope = gelu_parts(hidden)
        active = gelu_value.astype(jnp.bfloat16).astype(jnp.float32)
        d_active = jnp.einsum('ijc,hc->ijh', member_cot, outer_w)
        d_hidden = (d_active * gelu_slope).astype(jnp.bfloat16).astype(jnp.float32)
        d_state = member_cot + jnp.einsum('ijh,ch->ijc', d_hidden, inner_w)
        d_state_b = d_state.astype(jnp.bfloat16).astype(jnp.float32)
        outer_total = outer_total + jnp.einsum('ijh,ijc->hc', active, member_cot)
        inner_total = inner_total + jnp.einsum('ijc,ijh->ch', state_rows, d_hidden)
        filter_total = filter_total + jnp.einsum('kicj,ijd->kcd', filtered, d_state_b)
        d_filtered = jnp.einsum('ijd,kcd->kicj', d_state_b, filter_w).astype(jnp.bfloat16)
        d_basis = adjoint_rows(d_filtered, spectrum_real, spectrum_imag, tables).astype(jnp.float32)
        lat_part = jnp.einsum('kir,kicj->rjc', coupling, d_basis).astype(jnp.bfloat16).astype(jnp.float32)
        field_grads.append((d_state + lat_part).astype(jnp.bfloat16))
    field_grad = jnp.stack(field_grads, axis=0)
    return (field_grad, filter_total * grad_scale, inner_total * grad_scale, outer_total * grad_scale)
```

```python
import math

import jax
import jax.numpy as jnp
import ml_dtypes
import numpy as np
from jax import lax
from jax.experimental import pallas as pl
from jax.experimental.pallas import tpu as pltpu
from jax.sharding import PartitionSpec as P

GELU_SCALE = 0.7978845608028654
CUBIC_TERM = 0.044715
BF = jnp.bfloat16
F32 = jnp.float32
NLON = 1440
NZ = 8
LON = 180
MODES = 720
MP = 768
KP = 1536
CB = 16
NK = 3
NR = 4
LIMIT = 48 * 1024 * 1024


def dft_table():
    lane = np.arange(KP)
    tail = lane >= NZ * 128
    owner = np.where(tail, 2 * ((lane - NZ * 128) // 128) + (lane % 128 >= 64), lane // 128)
    place = np.where(tail, 128 + lane % 64, lane % 128)
    column = owner * LON + place
    frequency = np.arange(MP)
    phase = 2.0 * math.pi * ((column[:, None] * frequency[None, :]) % NLON) / NLON
    valid = (place < LON)[:, None] & (frequency < MODES)[None, :]
    table = np.concatenate(
        [np.where(valid, np.cos(phase), 0.0), np.where(valid, -np.sin(phase), 0.0)], axis=1
    )
    return table.astype(ml_dtypes.bfloat16)


def point_select():
    lane = np.arange(384)
    tile = lane // 128
    upper = np.where(tile == 1, lane % 128 >= 64, tile == 2).astype(np.int64)
    place = np.where(tile == 1, 128 + lane % 64, lane % 128)
    out = np.zeros((LON * NR, 2 * 384), np.float32)
    for first in range(2):
        row = 2 * upper + first
        good = place < LON
        out[(place * NR + row)[good], first * 384 + lane[good]] = 1.0
    return out.astype(ml_dtypes.bfloat16)


def dot(a, b):
    return jnp.dot(a, b, preferred_element_type=F32)


def dot_tn(a, b):
    return lax.dot_general(a, b, (((0,), (0,)), ((), ())), preferred_element_type=F32)


def dot_nt(a, b):
    return lax.dot_general(a, b, (((1,), (1,)), ((), ())), preferred_element_type=F32)


def low_halves(a, b):
    return jnp.concatenate([a[:, :64], b[:, :64]], axis=1)


def high_halves(a, b):
    return jnp.concatenate([a[:, 64:], b[:, 64:]], axis=1)


def unpack(ref, x_ref, base, rows):
    for z in range(NZ):
        lanes = slice(128 * z, 128 * z + 128)
        x_ref[base : base + rows, lanes] = ref[z, :rows, 0:128]
        x_ref[base + rows : base + 2 * rows, lanes] = ref[z, :rows, 256:384]
    for pair in range(NZ // 2):
        lanes = slice(128 * (NZ + pair), 128 * (NZ + pair) + 128)
        even = ref[2 * pair, :rows, 128:256]
        odd = ref[2 * pair + 1, :rows, 128:256]
        x_ref[base : base + rows, lanes] = low_halves(even, odd)
        x_ref[base + rows : base + 2 * rows, lanes] = high_halves(even, odd)


def pack(ref, tile, value, rows):
    lower, upper = value[:rows], value[rows : 2 * rows]
    if tile < NZ:
        ref[tile, :rows, 0:128] = lower
        ref[tile, :rows, 256:384] = upper
    else:
        pair = tile - NZ
        ref[2 * pair, :rows, 128:256] = low_halves(lower, upper)
        ref[2 * pair + 1, :rows, 128:256] = high_halves(lower, upper)


def coupling_matrix(weights):
    size = 12 * CB
    rows = lax.broadcasted_iota(jnp.int32, (size, 128), 0)
    cols = lax.broadcasted_iota(jnp.int32, (size, 128), 1)
    expand = (rows // CB == cols).astype(F32).astype(BF)
    wide = dot_nt(dot(expand, weights).astype(BF), expand)
    left = lax.broadcasted_iota(jnp.int32, (size, size), 0)
    right = lax.broadcasted_iota(jnp.int32, (size, size), 1)
    return jnp.where(left % CB == right % CB, wide, 0.0).astype(BF)


def pack_kernel(points_ref, select_ref, wide_ref, send_ref):
    wide = dot_tn(points_ref[...], select_ref[...]).astype(BF)
    wide_ref[...] = wide
    for s in range(NZ):
        for first in range(2):
            send_ref[s, CB * first : CB * first + CB, :] = wide[
                CB * s : CB * s + CB, 384 * first : 384 * first + 384
            ]


def turn_kernel(points_ref, select_ref, wide_ref):
    wide_ref[...] = dot_tn(points_ref[...], select_ref[...]).astype(BF)


def spectral(x, table_ref, gain_ref, filt_ref, sign):
    for q in range(MP // 256):
        lanes = slice(256 * q, 256 * q + 256)
        upper = slice(MP + 256 * q, MP + 256 * q + 256)
        part_a = dot(x, table_ref[:, lanes])
        part_b = dot(x, table_ref[:, upper])
        for g in range(12):
            rows = slice(CB * g, CB * g + CB)
            real = gain_ref[g : g + 1, lanes]
            imag = sign * gain_ref[12 + g : 13 + g, lanes]
            filt_ref[rows, lanes] = (real * part_a[rows] - imag * part_b[rows]).astype(BF)
            filt_ref[rows, upper] = (real * part_b[rows] + imag * part_a[rows]).astype(BF)


def filter_kernel(
    low_ref, own_ref, high_ref, weights_ref, gain_ref, table_ref, send_ref, x_ref, filt_ref
):
    for band, ref in enumerate((low_ref, own_ref, high_ref)):
        unpack(ref, x_ref, 64 * band, 32)
    basis = dot(coupling_matrix(weights_ref[...]), x_ref[...]).astype(BF)
    spectral(basis, table_ref, gain_ref, filt_ref, 1.0)
    for q in range(KP // 256):
        rows = slice(256 * q, 256 * q + 256)
        result = (dot_nt(filt_ref[...], table_ref[rows, :]) * (2.0 / NLON)).astype(BF)
        pack(send_ref, 2 * q, result[:, :128], 96)
        pack(send_ref, 2 * q + 1, result[:, 128:], 96)


def gelu_parts(hidden):
    inner_part = GELU_SCALE * (hidden + CUBIC_TERM * hidden * hidden * hidden)
    tangent = jnp.tanh(inner_part)
    gelu_value = 0.5 * hidden * (1.0 + tangent)
    gelu_slope = 0.5 * (1.0 + tangent) + 0.5 * hidden * (1.0 - tangent * tangent) * GELU_SCALE * (
        1.0 + 3.0 * CUBIC_TERM * hidden * hidden
    )
    return (gelu_value, gelu_slope)


def mlp_kernel(
    recv_ref,
    fields_ref,
    cot_ref,
    filter_ref,
    inner_ref,
    outer_ref,
    send_ref,
    state_grad_ref,
    grads_ref,
):
    mix = jnp.concatenate(
        [filter_ref[k, CB * s : CB * s + CB, :] for s in range(NZ) for k in range(NK)], axis=0
    )
    inner = inner_ref[...]
    outer = outer_ref[...]
    sums = None
    for first in range(2):
        lanes = slice(384 * first, 384 * first + 384)
        filtered = jnp.concatenate(
            [recv_ref[s, 48 * first : 48 * first + 48, :] for s in range(NZ)], axis=0
        )
        cot = cot_ref[:, lanes]
        state = (fields_ref[:, lanes].astype(F32) + dot_tn(mix, filtered)).astype(BF)
        hidden = dot_tn(inner, state)
        value, slope = gelu_parts(hidden)
        active = value.astype(BF)
        d_hidden = (dot(outer, cot) * slope).astype(BF)
        d_state = cot.astype(F32) + dot(inner, d_hidden)
        state_grad_ref[:, lanes] = d_state
        d_state_b = d_state.astype(BF)
        d_filtered = dot(mix, d_state_b).astype(BF)
        for s in range(NZ):
            send_ref[s, 48 * first : 48 * first + 48, :] = d_filtered[48 * s : 48 * s + 48]
        parts = (dot_nt(filtered, d_state_b), dot_nt(active, cot), dot_nt(state, d_hidden))
        sums = parts if sums is None else tuple(a + b for a, b in zip(sums, parts))
    grads_ref[0:384, :] = sums[0].astype(BF)
    grads_ref[384:640, :] = sums[1].astype(BF)
    grads_ref[640:768, :] = sums[2][:, :128].astype(BF)
    grads_ref[768:896, :] = sums[2][:, 128:].astype(BF)
    for s in range(NZ):
        chunk_out(send_ref, s, 96, grads_ref[112 * s : 112 * s + 112, :])


def chunk_out(ref, s, base, chunk):
    ref[s, base : base + 48, 0:128] = chunk[0:48]
    ref[s, base : base + 48, 128:256] = chunk[48:96]
    ref[s, base : base + 16, 256:384] = chunk[96:112]
    ref[s, base + 16 : base + 48, 256:384] = jnp.zeros((32, 128), BF)


def chunk_sum_kernel(recv_ref, out_ref):
    total = recv_ref[0].astype(F32)
    for z in range(1, NZ):
        total = total + recv_ref[z].astype(F32)
    total = total.astype(BF)
    out_ref[0:48, :] = total[:, 0:128]
    out_ref[48:96, :] = total[:, 128:256]
    out_ref[96:128, :] = total[0:32, 256:384]


def adjoint_kernel(
    recv_ref,
    weights_ref,
    gain_ref,
    table_ref,
    low_ref,
    own_ref,
    high_ref,
    x_ref,
    filt_ref,
):
    unpack(recv_ref, x_ref, 0, 96)
    spectral(x_ref[...], table_ref, gain_ref, filt_ref, -1.0)
    coupling = coupling_matrix(weights_ref[...])
    for q in range(KP // 256):
        rows = slice(256 * q, 256 * q + 256)
        result = (dot_nt(filt_ref[...], table_ref[rows, :]) * (2.0 / NLON)).astype(BF)
        parts = dot(coupling, result)
        for half in range(2):
            lanes = slice(128 * half, 128 * half + 128)
            pack(low_ref, 2 * q + half, parts[0:64, lanes].astype(BF), 32)
            pack(own_ref, 2 * q + half, parts[64:128, lanes], 32)
            pack(high_ref, 2 * q + half, parts[128:192, lanes].astype(BF), 32)


def halo_sum_kernel(own_ref, from_high_ref, from_low_ref, chunk_ref, send_ref):
    chunk = chunk_ref[...]
    for z in range(NZ):
        total = own_ref[z] + from_high_ref[z].astype(F32) + from_low_ref[z].astype(F32)
        send_ref[z, 0:32, :] = total.astype(BF)
        chunk_out(send_ref, z, 32, chunk)


def finish_kernel(scale, recv_ref, state_grad_ref, select_ref, grad_ref, filter_ref, inner_ref, outer_ref, all_ref):
    for first in range(2):
        lanes = slice(384 * first, 384 * first + 384)
        lat_part = jnp.concatenate(
            [recv_ref[s, CB * first : CB * first + CB, :] for s in range(NZ)], axis=0
        )
        total = (state_grad_ref[:, lanes] + lat_part.astype(F32)).astype(BF)
        part = dot_nt(select_ref[:, lanes], total)
        if first == 0:
            held = part
        else:
            grad_ref[...] = (held + part).astype(BF)
    for s in range(NZ):
        base = 112 * s
        all_ref[base : base + 48, :] = recv_ref[s, 32:80, 0:128].astype(F32) * scale
        all_ref[base + 48 : base + 96, :] = recv_ref[s, 32:80, 128:256].astype(F32) * scale
        all_ref[base + 96 : base + 112, :] = recv_ref[s, 32:48, 256:384].astype(F32) * scale
    for s in range(NZ):
        for k in range(NK):
            base = 48 * s + CB * k
            filter_ref[k, CB * s : CB * s + CB, :] = all_ref[base : base + CB, :]
    outer_ref[...] = all_ref[384:640, :]
    inner_ref[:, :128] = all_ref[640:768, :]
    inner_ref[:, 128:] = all_ref[768:896, :]


def call(kernel, outs, flops, scratch=(), in_specs=None):
    single = not isinstance(outs, (list, tuple))
    shapes = [outs] if single else list(outs)
    moved = sum(math.prod(o.shape) * o.dtype.itemsize for o in shapes)
    run = pl.pallas_call(
        kernel,
        out_shape=outs,
        in_specs=in_specs,
        out_specs=jax.tree.map(lambda _: pl.BlockSpec(memory_space=pltpu.VMEM), outs),
        scratch_shapes=scratch,
        compiler_params=pltpu.CompilerParams(vmem_limit_bytes=LIMIT),
        cost_estimate=pl.CostEstimate(flops=flops, bytes_accessed=2 * moved, transcendentals=0),
    )
    return run


def shaped(shape, dtype=BF):
    return jax.ShapeDtypeStruct(shape, dtype)


def vmem(count):
    return [pl.BlockSpec(memory_space=pltpu.VMEM)] * count


def shifted(value, axis, steps):
    count = lax.axis_size(axis)
    leading, last = (max(0, -steps), min(count, count - steps))
    return lax.ppermute(value, axis, [(source, source + steps) for source in range(leading, last)])


def local(
    fields,
    cotangent,
    basis_weights,
    band_support,
    spectrum_real,
    spectrum_imag,
    filter_weights,
    inner_weights,
    outer_weights,
):
    group = lax.axis_size("ens") * lax.axis_size("lat")
    grad_scale = 1.0 / math.sqrt(group * NR * NLON)
    table = jnp.asarray(dft_table())
    select = jnp.asarray(point_select())

    field_points = fields[0].transpose(1, 0, 2).reshape(LON * NR, 128)
    cot_points = cotangent[0].transpose(1, 0, 2).reshape(LON * NR, 128)
    field_wide, send_fields = call(
        pack_kernel, (shaped((128, 768)), shaped((NZ, 32, 384))), 2 * 720 * 768 * 128, (), vmem(2)
    )(field_points, select)
    own = lax.all_to_all(send_fields, "lon", 0, 0, tiled=True)

    cot_wide = call(turn_kernel, shaped((128, 768)), 2 * 720 * 768 * 128, (), vmem(2))(
        cot_points, select
    )
    mask = jnp.repeat(band_support[0], NR).astype(BF)
    masked = (basis_weights * mask[None, None, :]).transpose(1, 0, 2).reshape(12, 12)
    weights = jnp.pad(masked, ((0, 116), (0, 116)))
    weights_t = jnp.pad(masked.T, ((0, 116), (0, 116)))
    first_half = jnp.where(jnp.arange(MODES) == 0, 0.5, 1.0).astype(F32)
    gains = jnp.concatenate(
        [
            (s * first_half).transpose(1, 0, 2).reshape(12, MODES)
            for s in (spectrum_real, spectrum_imag)
        ],
        axis=0,
    )
    gains = jnp.pad(gains, ((0, 0), (0, MP - MODES)))

    low = shifted(own, "lat", 1)
    high = shifted(own, "lat", -1)
    work = [pltpu.VMEM((192, KP), BF), pltpu.VMEM((192, KP), BF)]
    send_filtered = call(
        filter_kernel, shaped((NZ, 96, 384)), 4 * 192 * KP * KP, work, vmem(6)
    )(low, own, high, weights, gains, table)
    filtered = lax.all_to_all(send_filtered, "lon", 0, 0, tiled=True)

    send_back, state_grad = call(
        mlp_kernel,
        (shaped((NZ, 144, 384)), shaped((128, 768), F32)),
        2 * 768 * 128 * 256 * 10,
        [pltpu.VMEM((896, 128), BF)],
        vmem(6),
    )(filtered, field_wide, cot_wide, filter_weights, inner_weights, outer_weights)
    back = lax.all_to_all(send_back, "lon", 0, 0, tiled=True)

    chunk = pl.pallas_call(
        chunk_sum_kernel,
        grid=(1,),
        in_specs=[pl.BlockSpec((NZ, 48, 384), lambda i: (0, 2, 0))],
        out_specs=pl.BlockSpec((128, 128), lambda i: (0, 0)),
        out_shape=shaped((128, 128)),
        cost_estimate=pl.CostEstimate(flops=150000, bytes_accessed=400000, transcendentals=0),
    )(back)
    share = 128 // group
    ids = np.arange(128) % share
    same = jnp.asarray((ids[:, None] == ids[None, :]).astype(ml_dtypes.bfloat16))
    chunk = lax.all_to_all(chunk, ("ens", "lat"), 0, 0, tiled=True)
    chunk = dot(same, chunk).astype(BF)
    chunk = lax.all_to_all(chunk, ("ens", "lat"), 0, 0, tiled=True)

    to_low, kept, to_high = call(
        adjoint_kernel,
        (shaped((NZ, 32, 384)), shaped((NZ, 32, 384), F32), shaped((NZ, 32, 384))),
        4 * 192 * KP * KP,
        work,
        vmem(4),
    )(back, weights_t, gains, table)
    from_high = shifted(to_low, "lat", -1)
    from_low = shifted(to_high, "lat", 1)
    send_lat = call(halo_sum_kernel, shaped((NZ, 80, 384)), 300000, (), vmem(4))(
        kept, from_high, from_low, chunk
    )
    lat_parts = lax.all_to_all(send_lat, "lon", 0, 0, tiled=True)

    def finish(*refs):
        finish_kernel(grad_scale, *refs)

    grad_points, filter_grad, inner_grad, outer_grad = call(
        finish,
        (
            shaped((LON * NR, 128)),
            shaped((NK, 128, 128), F32),
            shaped((128, 256), F32),
            shaped((256, 128), F32),
        ),
        2 * 720 * 768 * 128,
        [pltpu.VMEM((896, 128), F32)],
        vmem(3),
    )(lat_parts, state_grad, select)
    field_grad = grad_points.reshape(LON, NR, 128).transpose(1, 0, 2)[None]
    return (field_grad, filter_grad, inner_grad, outer_grad)


def solution(mesh):
    placed = (
        P("ens", "lat", "lon", None),
        P("ens", "lat", "lon", None),
        P(None, "lat", None),
        P("lat", None),
        P(None, "lat", None),
        P(None, "lat", None),
        P(),
        P(),
        P(),
    )
    return jax.shard_map(
        local,
        mesh=mesh,
        in_specs=placed,
        out_specs=(P("ens", "lat", "lon", None), P(), P(), P()),
        check_vma=False,
    )
```

```python
import math

import jax
import jax.numpy as jnp
import ml_dtypes
import numpy as np
from jax import lax
from jax.experimental import pallas as pl
from jax.experimental.pallas import tpu as pltpu
from jax.sharding import PartitionSpec as P

GELU_SCALE = 0.7978845608028654
CUBIC_TERM = 0.044715
BF = jnp.bfloat16
F32 = jnp.float32
NLON = 1440
NZ = 8
LON = 180
MODES = 720
MP = 384
KP = 768
CB = 16
NK = 3
NR = 4
WIDE = 1024
LIMIT = 24 * 1024 * 1024


def dft_table():
    lane = np.arange(KP)
    tail = lane >= 512
    owner = np.where(tail, 2 * ((lane - 512) // 128) + (lane % 128 >= 64), lane // 128)
    place = np.where(tail, 128 + lane % 64, lane % 128)
    column = owner * LON + place
    tables = []
    for parity in range(2):
        frequency = 2 * np.arange(MP) + parity
        phase = 2.0 * math.pi * ((column[:, None] * frequency[None, :]) % NLON) / NLON
        valid = (place < LON)[:, None] & (frequency < MODES)[None, :]
        cos = np.where(valid, np.cos(phase), 0.0)
        sin = np.where(valid, -np.sin(phase), 0.0)
        tables.append(np.concatenate([cos, sin], axis=1))
    return np.stack(tables).astype(ml_dtypes.bfloat16)


def dot(a, b):
    return jnp.dot(a, b, preferred_element_type=F32)


def dot_tn(a, b):
    return lax.dot_general(a, b, (((0,), (0,)), ((), ())), preferred_element_type=F32)


def dot_nt(a, b):
    return lax.dot_general(a, b, (((1,), (1,)), ((), ())), preferred_element_type=F32)


def low_halves(a, b):
    return jnp.concatenate([a[:, :64], b[:, :64]], axis=1)


def high_halves(a, b):
    return jnp.concatenate([a[:, 64:], b[:, 64:]], axis=1)


def iota(shape, dim):
    return lax.broadcasted_iota(jnp.int32, shape, dim)


def point_select():
    lane = iota((8, 2 * 384), 1)
    first = (lane >= 384).astype(jnp.int32)
    lane = lane - 384 * first
    middle = (lane >= 128) & (lane < 256)
    upper = ((lane >= 192)).astype(jnp.int32)
    place = jnp.where(middle, 128 + (lane & 63), lane & 127)
    point = jnp.where(place < LON, place * NR + 2 * upper + first, -1)
    return (iota((LON * NR, 2 * 384), 0) == point[0:1]).astype(F32).astype(BF)


def tile_of(z):
    return 6 * (z // 4) + z % 4


def tile_of_pair(pair):
    return 6 * (pair // 2) + 4 + pair % 2


def unpack(ref, x_ref, base, rows):
    for z in range(NZ):
        lanes = slice(128 * tile_of(z), 128 * tile_of(z) + 128)
        x_ref[base : base + rows, lanes] = ref[z, :, 0:128]
        x_ref[base + rows : base + 2 * rows, lanes] = ref[z, :, 256:384]
    for pair in range(NZ // 2):
        lanes = slice(128 * tile_of_pair(pair), 128 * tile_of_pair(pair) + 128)
        even = ref[2 * pair, :, 128:256]
        odd = ref[2 * pair + 1, :, 128:256]
        x_ref[base : base + rows, lanes] = low_halves(even, odd)
        x_ref[base + rows : base + 2 * rows, lanes] = high_halves(even, odd)


def pack(ref, half, value, rows):
    for t in range(4):
        lanes = slice(128 * t, 128 * t + 128)
        ref[4 * half + t, :, 0:128] = value[:rows, lanes]
        ref[4 * half + t, :, 256:384] = value[rows:, lanes]
    for t in range(2):
        lanes = slice(512 + 128 * t, 640 + 128 * t)
        lower, upper = value[:rows, lanes], value[rows:, lanes]
        ref[4 * half + 2 * t, :, 128:256] = low_halves(lower, upper)
        ref[4 * half + 2 * t + 1, :, 128:256] = high_halves(lower, upper)


def bring(pairs, sems):
    copies = [
        pltpu.make_async_copy(source, target, sems.at[n]) for n, (source, target) in enumerate(pairs)
    ]
    for copy in copies:
        copy.start()
    return copies


def pack_kernel(points_hbm, wide_ref, send_ref, points_ref, sems):
    copies = bring([(points_hbm, points_ref)], sems)
    select = point_select()
    copies[0].wait()
    wide = dot_tn(points_ref[...], select).astype(BF)
    wide_ref[...] = wide
    for s in range(NZ):
        for first in range(2):
            send_ref[s, CB * first : CB * first + CB, :] = wide[
                CB * s : CB * s + CB, 384 * first : 384 * first + 384
            ]


def prepare_kernel(
    points_hbm,
    weights_hbm,
    real_hbm,
    imag_hbm,
    support_hbm,
    wide_ref,
    coupling_ref,
    turned_hbm,
    gain_ref,
    turned_ref,
    points_ref,
    weights_ref,
    real_ref,
    imag_ref,
    support_ref,
    sems,
):
    copies = bring(
        (
            (points_hbm, points_ref),
            (weights_hbm, weights_ref),
            (real_hbm, real_ref),
            (imag_hbm, imag_ref),
            (support_hbm, support_ref),
        ),
        sems,
    )
    select = point_select()
    copies[0].wait()
    wide_ref[...] = dot_tn(points_ref[...], select).astype(BF)

    for copy in copies[1:]:
        copy.wait()
    flip = lax.rem(lax.axis_index("lat"), 2) == 0
    lane = iota((1, 12), 1)
    seen = support_ref[...]
    seen = jnp.where(lane < 4, seen[:, 0:1], jnp.where(lane < 8, seen[:, 1:2], seen[:, 2:3]))
    seen = seen.astype(F32)
    rows = [weights_ref[k].astype(F32) for k in range(NK)]
    masked = jnp.concatenate([rows[k][i : i + 1] * seen for i in range(NR) for k in range(NK)], axis=0)
    turned = jnp.concatenate([masked[:, 8:12], masked[:, 4:8], masked[:, 0:4]], axis=1)
    masked = jnp.where(flip, turned, masked).astype(BF)
    size = 12 * CB
    expand = (iota((size, 12), 0) // CB == iota((size, 12), 1)).astype(F32).astype(BF)
    same = (iota((size, size), 0) & 15) == (iota((size, size), 1) & 15)
    wide = dot_nt(dot(expand, masked).astype(BF), expand)
    coupling_ref[...] = jnp.where(same, wide, 0.0).astype(BF)
    wide = dot_nt(dot_nt(expand, masked).astype(BF), expand)
    turned_ref[...] = jnp.where(same, wide, 0.0).astype(BF)
    copies = bring([(turned_ref, turned_hbm)], sems)

    lane = iota((MODES, 2 * MP), 1)
    odd = (lane >= MP).astype(jnp.int32)
    split = (iota((MODES, 2 * MP), 0) == 2 * (lane - MP * odd) + odd).astype(F32).astype(BF)
    first_half = jnp.where(iota((1, 2 * MP), 1) == 0, 0.5, 1.0).astype(F32)
    for part, ref in enumerate((real_ref, imag_ref)):
        rows = [ref[k] for k in range(NK)]
        rest = jnp.concatenate([rows[k][i : i + 1] for i in range(NR) for k in range(NK)], axis=0)
        moved = None
        for step in range(3):
            piece = rest.astype(BF)
            rest = rest - piece.astype(F32)
            term = dot(piece, split)
            moved = term if moved is None else moved + term
        gain_ref[12 * part : 12 * part + 12, :] = moved * first_half
    copies[0].wait()


def spectral(value, parity, table_ref, gain_ref, filt_ref, sign):
    spec = dot(value, table_ref[parity])
    lanes = slice(MP * parity, MP * parity + MP)
    for g in range(12):
        rows = slice(CB * g, CB * g + CB)
        part_a, part_b = spec[rows, :MP], spec[rows, MP:]
        real = gain_ref[g : g + 1, lanes]
        imag = sign * gain_ref[12 + g : 13 + g, lanes]
        filt_ref[parity, rows, :MP] = (real * part_a - imag * part_b).astype(BF)
        filt_ref[parity, rows, MP:] = (real * part_b + imag * part_a).astype(BF)


def transform(lower, upper, table_ref, gain_ref, filt_ref, sign, copies):
    for parity, value in enumerate((lower + upper, lower - upper)):
        copies[parity].wait()
        spectral(value.astype(BF), parity, table_ref, gain_ref, filt_ref, sign)
    even = dot_nt(filt_ref[0], table_ref[0])
    odd = dot_nt(filt_ref[1], table_ref[1])
    scale = 2.0 / NLON
    return ((even + odd) * scale).astype(BF), ((even - odd) * scale).astype(BF)


def filter_kernel(
    first_ref,
    own_ref,
    second_ref,
    coupling_ref,
    gain_ref,
    table_hbm,
    send_ref,
    x_ref,
    filt_ref,
    table_ref,
    sems,
):
    copies = bring([(table_hbm.at[p], table_ref.at[p]) for p in range(2)], sems)
    for band, ref in enumerate((first_ref, own_ref, second_ref)):
        unpack(ref, x_ref, 64 * band, 32)
    coupling = coupling_ref[...]
    lower = dot(coupling, x_ref[:, :KP])
    upper = dot(coupling, x_ref[:, KP:])
    lower, upper = transform(lower, upper, table_ref, gain_ref, filt_ref, 1.0, copies)
    pack(send_ref, 0, lower, 96)
    pack(send_ref, 1, upper, 96)


def gelu_parts(hidden):
    inner_part = GELU_SCALE * (hidden + CUBIC_TERM * hidden * hidden * hidden)
    tangent = jnp.tanh(inner_part)
    gelu_value = 0.5 * hidden * (1.0 + tangent)
    gelu_slope = 0.5 * (1.0 + tangent) + 0.5 * hidden * (1.0 - tangent * tangent) * GELU_SCALE * (
        1.0 + 3.0 * CUBIC_TERM * hidden * hidden
    )
    return (gelu_value, gelu_slope)


def mlp_kernel(
    recv_ref,
    fields_ref,
    cot_ref,
    filter_ref,
    inner_ref,
    outer_ref,
    send_ref,
    state_grad_hbm,
    grads_hbm,
    state_grad_ref,
    grads_ref,
    sems,
):
    mix = jnp.concatenate(
        [filter_ref[k, CB * s : CB * s + CB, :] for s in range(NZ) for k in range(NK)], axis=0
    )
    inner = inner_ref[...]
    outer = outer_ref[...]
    sums = None
    for first in range(2):
        lanes = slice(384 * first, 384 * first + 384)
        filtered = jnp.concatenate(
            [recv_ref[s, 48 * first : 48 * first + 48, :] for s in range(NZ)], axis=0
        )
        cot = cot_ref[:, lanes]
        state = (fields_ref[:, lanes].astype(F32) + dot_tn(mix, filtered)).astype(BF)
        hidden = dot_tn(inner, state)
        value, slope = gelu_parts(hidden)
        active = value.astype(BF)
        d_hidden = (dot(outer, cot) * slope).astype(BF)
        d_state = cot.astype(F32) + dot(inner, d_hidden)
        state_grad_ref[:, lanes] = d_state
        d_state_b = d_state.astype(BF)
        d_filtered = dot(mix, d_state_b).astype(BF)
        for s in range(NZ):
            send_ref[s, 48 * first : 48 * first + 48, :] = d_filtered[48 * s : 48 * s + 48]
        parts = (dot_nt(filtered, d_state_b), dot_nt(active, cot), dot_nt(state, d_hidden))
        sums = parts if sums is None else tuple(a + b for a, b in zip(sums, parts))
    grads_ref[0:384, :] = sums[0].astype(BF)
    grads_ref[384:640, :] = sums[1].astype(BF)
    grads_ref[640:768, :] = sums[2][:, :128].astype(BF)
    grads_ref[768:896, :] = sums[2][:, 128:].astype(BF)
    grads_ref[896:WIDE, :] = jnp.zeros((WIDE - 896, 128), BF)
    for copy in bring(((grads_ref, grads_hbm), (state_grad_ref, state_grad_hbm)), sems):
        copy.wait()


def adjoint_kernel(
    recv_ref,
    coupling_hbm,
    gain_ref,
    table_hbm,
    first_ref,
    own_hbm,
    second_ref,
    coupling_ref,
    own_ref,
    x_ref,
    filt_ref,
    table_ref,
    sems,
):
    copies = bring(
        [(table_hbm.at[p], table_ref.at[p]) for p in range(2)] + [(coupling_hbm, coupling_ref)], sems
    )
    unpack(recv_ref, x_ref, 0, 96)
    lower = x_ref[:, :KP].astype(F32)
    upper = x_ref[:, KP:].astype(F32)
    halves = transform(lower, upper, table_ref, gain_ref, filt_ref, -1.0, copies)
    copies[2].wait()
    coupling = coupling_ref[...]
    for half, value in enumerate(halves):
        parts = dot(coupling, value)
        pack(first_ref, half, parts[0:64].astype(BF), 32)
        pack(own_ref, half, parts[64:128], 32)
        pack(second_ref, half, parts[128:192].astype(BF), 32)
    bring([(own_ref, own_hbm)], sems)[0].wait()


def halo_sum_kernel(own_hbm, first_ref, second_ref, chunks_ref, send_ref, own_ref, sems):
    copies = bring([(own_hbm, own_ref)], sems)
    chunk = chunks_ref[0].astype(F32)
    for n in range(1, chunks_ref.shape[0]):
        chunk = chunk + chunks_ref[n].astype(F32)
    chunk = chunk.astype(BF)
    size = chunk.shape[0]
    copies[0].wait()
    for z in range(NZ):
        total = own_ref[z] + first_ref[z].astype(F32) + second_ref[z].astype(F32)
        total = total.astype(BF)
        for tile in range(3):
            send_ref[z, 32 * tile : 32 * tile + 32, :] = total[:, 128 * tile : 128 * tile + 128]
        send_ref[z, 96 : 96 + size, :] = chunk


def chunk_sum_kernel(recv_ref, out_ref):
    size = recv_ref.shape[1] - 96
    total = recv_ref[0, 96:, :].astype(F32)
    for z in range(1, NZ):
        total = total + recv_ref[z, 96:, :].astype(F32)
    total = total.astype(BF)
    for n in range(WIDE // size):
        out_ref[size * n : size * n + size, :] = total


def field_kernel(recv_ref, state_grad_ref, grad_ref):
    totals = []
    for first in range(2):
        tiles = []
        for tile in range(3):
            base = 32 * tile + CB * first
            tiles.append(
                jnp.concatenate([recv_ref[s, base : base + CB, :] for s in range(NZ)], axis=0)
            )
        lat_part = jnp.concatenate(tiles, axis=1).astype(F32)
        total = state_grad_ref[:, 384 * first : 384 * first + 384] + lat_part
        totals.append(total.astype(BF))
    grad_ref[...] = dot_nt(point_select(), jnp.concatenate(totals, axis=1)).astype(BF)


def weights_kernel(scale, grads_ref, filter_ref, inner_ref, outer_ref):
    for s in range(NZ):
        for k in range(NK):
            base = 48 * s + CB * k
            filter_ref[k, CB * s : CB * s + CB, :] = grads_ref[base : base + CB, :].astype(F32) * scale
    outer_ref[...] = grads_ref[384:640, :].astype(F32) * scale
    inner_ref[:, :128] = grads_ref[640:768, :].astype(F32) * scale
    inner_ref[:, 128:] = grads_ref[768:896, :].astype(F32) * scale


def call(kernel, outs, flops, scratch=(), in_specs=None, out_specs=None):
    shapes = outs if isinstance(outs, tuple) else (outs,)
    moved = sum(math.prod(o.shape) * o.dtype.itemsize for o in shapes)
    if out_specs is None:
        out_specs = jax.tree.map(lambda _: pl.BlockSpec(memory_space=pltpu.VMEM), outs)
    return pl.pallas_call(
        kernel,
        out_shape=outs,
        in_specs=in_specs,
        out_specs=out_specs,
        scratch_shapes=scratch,
        compiler_params=pltpu.CompilerParams(vmem_limit_bytes=LIMIT),
        cost_estimate=pl.CostEstimate(flops=flops, bytes_accessed=2 * moved, transcendentals=0),
    )


def shaped(shape, dtype=BF):
    return jax.ShapeDtypeStruct(shape, dtype)


def in_hbm(shape, dtype=BF):
    return pltpu.HBM(shape, dtype)


def hold(value):
    return pltpu.with_memory_space_constraint(value, pltpu.HBM)


def vmem(count):
    return [pl.BlockSpec(memory_space=pltpu.VMEM)] * count


def hbm(count):
    return [pl.BlockSpec(memory_space=pltpu.HBM)] * count


def swapped(value, first):
    count = lax.axis_size("lat")
    pairs = []
    for low in range(first, count - 1, 2):
        pairs += [(low, low + 1), (low + 1, low)]
    return lax.ppermute(value, "lat", pairs)


def local(
    fields,
    cotangent,
    basis_weights,
    band_support,
    spectrum_real,
    spectrum_imag,
    filter_weights,
    inner_weights,
    outer_weights,
):
    group = lax.axis_size("lat")
    grad_scale = 1.0 / math.sqrt(lax.axis_size("ens") * group * NR * NLON)
    table = hold(jnp.asarray(dft_table()))

    field_points = fields[0].transpose(1, 0, 2).reshape(LON * NR, 128)
    cot_points = cotangent[0].transpose(1, 0, 2).reshape(LON * NR, 128)
    field_wide, send_fields = call(
        pack_kernel, (shaped((128, 768)), shaped((NZ, 32, 384))), 2 * 720 * 768 * 128,
        [pltpu.VMEM((720, 128), BF), pltpu.SemaphoreType.DMA((1,))], hbm(1)
    )(hold(field_points))
    own = lax.all_to_all(send_fields, "lon", 0, 0, tiled=True)

    cot_wide, coupling, turned, gains = call(
        prepare_kernel,
        (
            shaped((128, 768)),
            shaped((192, 192)),
            in_hbm((192, 192)),
            shaped((24, 2 * MP), F32),
        ),
        2 * 720 * 768 * 128,
        [
            pltpu.VMEM((192, 192), BF),
            pltpu.VMEM((720, 128), BF),
            pltpu.VMEM((NK, NR, 12), BF),
            pltpu.VMEM((NK, NR, MODES), F32),
            pltpu.VMEM((NK, NR, MODES), F32),
            pltpu.VMEM((1, 3), jnp.int32),
            pltpu.SemaphoreType.DMA((5,)),
        ],
        hbm(5),
        tuple(vmem(2) + hbm(1) + vmem(1)),
    )(
        hold(cot_points),
        hold(basis_weights),
        hold(spectrum_real),
        hold(spectrum_imag),
        hold(band_support),
    )

    first = swapped(own, 0)
    second = swapped(own, 1)
    work = [
        pltpu.VMEM((192, 2 * KP), BF),
        pltpu.VMEM((2, 192, 2 * MP), BF),
        pltpu.VMEM((2, KP, 2 * MP), BF),
        pltpu.SemaphoreType.DMA((3,)),
    ]
    send_filtered = call(
        filter_kernel, shaped((NZ, 96, 384)), 8 * 192 * KP * KP, work, vmem(5) + hbm(1)
    )(first, own, second, coupling, gains, table)
    filtered = lax.all_to_all(send_filtered, "lon", 0, 0, tiled=True)

    send_back, state_grad, grads = call(
        mlp_kernel,
        (shaped((NZ, 96, 384)), in_hbm((128, 768), F32), in_hbm((WIDE, 128))),
        2 * 768 * 128 * 256 * 10,
        [
            pltpu.VMEM((128, 768), F32),
            pltpu.VMEM((WIDE, 128), BF),
            pltpu.SemaphoreType.DMA((2,)),
        ],
        vmem(6),
        tuple(vmem(1) + hbm(2)),
    )(filtered, field_wide, cot_wide, filter_weights, inner_weights, outer_weights)
    back = lax.all_to_all(send_back, "lon", 0, 0, tiled=True)
    grads_other = lax.ppermute(grads, "ens", [(0, 1), (1, 0)])
    grads = (grads.astype(F32) + grads_other.astype(F32)).astype(BF)
    share = WIDE // group
    chunks = lax.all_to_all(grads.reshape(group, share, 128), "lat", 0, 0, tiled=True)

    pieces = (NZ, 32, 384)
    to_first, kept, to_second = call(
        adjoint_kernel,
        (shaped(pieces), in_hbm(pieces, F32), shaped(pieces)),
        8 * 192 * KP * KP,
        [pltpu.VMEM((192, 192), BF), pltpu.VMEM(pieces, F32)] + work,
        vmem(1) + hbm(1) + vmem(1) + hbm(1),
        tuple(vmem(1) + hbm(1) + vmem(1)),
    )(back, hold(turned), gains, table)
    from_first = swapped(to_first, 0)
    from_second = swapped(to_second, 1)
    send_lat = call(
        halo_sum_kernel,
        shaped((NZ, 96 + share, 128)),
        300000,
        [pltpu.VMEM(pieces, F32), pltpu.SemaphoreType.DMA((1,))],
        hbm(1) + vmem(3),
    )(hold(kept), from_first, from_second, chunks)
    lat_parts = lax.all_to_all(send_lat, "lon", 0, 0, tiled=True)

    spread = call(chunk_sum_kernel, shaped((WIDE, 128)), 40000, (), vmem(1))(lat_parts)
    gathered = lax.all_to_all(spread.reshape(group, share, 128), "lat", 0, 0, tiled=True)
    grad_points = call(field_kernel, shaped((LON * NR, 128)), 2 * 720 * 768 * 128, (), vmem(2))(
        lat_parts, hold(state_grad)
    )

    def weights(*refs):
        weights_kernel(grad_scale, *refs)

    filter_grad, inner_grad, outer_grad = call(
        weights,
        (shaped((NK, 128, 128), F32), shaped((128, 256), F32), shaped((256, 128), F32)),
        WIDE * 128,
        (),
        vmem(1),
    )(gathered.reshape(WIDE, 128))
    field_grad = grad_points.reshape(LON, NR, 128).transpose(1, 0, 2)[None]
    return (field_grad, filter_grad, inner_grad, outer_grad)


def solution(mesh):
    placed = (
        P("ens", "lat", "lon", None),
        P("ens", "lat", "lon", None),
        P(None, "lat", None),
        P("lat", None),
        P(None, "lat", None),
        P(None, "lat", None),
        P(),
        P(),
        P(),
    )
    return jax.shard_map(
        local,
        mesh=mesh,
        in_specs=placed,
        out_specs=(P("ens", "lat", "lon", None), P(), P(), P()),
        check_vma=False,
    )
```

```python
import functools
import math

import jax
import jax.numpy as jnp
import ml_dtypes
import numpy as np
from jax import lax
from jax.experimental import pallas as pl
from jax.experimental.pallas import tpu as pltpu
from jax.sharding import PartitionSpec as P

GELU_SCALE = 0.7978845608028654
CUBIC_TERM = 0.044715
BF = jnp.bfloat16
F32 = jnp.float32
NLON = 1440
NZ = 8
LON = 180
MODES = 720
MP = 384
KP = 768
CB = 16
NK = 3
NR = 4
WIDE = 1024
LIMIT = 24 * 1024 * 1024


def dft_table():
    lane = np.arange(KP)
    tail = lane >= 512
    owner = np.where(tail, 2 * ((lane - 512) // 128) + (lane % 128 >= 64), lane // 128)
    place = np.where(tail, 128 + lane % 64, lane % 128)
    column = owner * LON + place
    tables = []
    for parity in range(2):
        frequency = 2 * np.arange(MP) + parity
        phase = 2.0 * math.pi * ((column[:, None] * frequency[None, :]) % NLON) / NLON
        valid = (place < LON)[:, None] & (frequency < MODES)[None, :]
        cos = np.where(valid, np.cos(phase), 0.0)
        sin = np.where(valid, -np.sin(phase), 0.0)
        tables.append(np.concatenate([cos, sin], axis=1))
    return np.stack(tables).astype(ml_dtypes.bfloat16)


def dot(a, b):
    return jnp.dot(a, b, preferred_element_type=F32)


def dot_tn(a, b):
    return lax.dot_general(a, b, (((0,), (0,)), ((), ())), preferred_element_type=F32)


def dot_nt(a, b):
    return lax.dot_general(a, b, (((1,), (1,)), ((), ())), preferred_element_type=F32)


def low_halves(a, b):
    return jnp.concatenate([a[:, :64], b[:, :64]], axis=1)


def high_halves(a, b):
    return jnp.concatenate([a[:, 64:], b[:, 64:]], axis=1)


def iota(shape, dim):
    return lax.broadcasted_iota(jnp.int32, shape, dim)


def point_select():
    lane = iota((8, 2 * 384), 1)
    first = (lane >= 384).astype(jnp.int32)
    lane = lane - 384 * first
    middle = (lane >= 128) & (lane < 256)
    upper = ((lane >= 192)).astype(jnp.int32)
    place = jnp.where(middle, 128 + (lane & 63), lane & 127)
    point = jnp.where(place < LON, place * NR + 2 * upper + first, -1)
    return (iota((LON * NR, 2 * 384), 0) == point[0:1]).astype(F32).astype(BF)


def tile_of(z):
    return 6 * (z // 4) + z % 4


def tile_of_pair(pair):
    return 6 * (pair // 2) + 4 + pair % 2


def unpack(ref, x_ref, base, rows):
    for z in range(NZ):
        lanes = slice(128 * tile_of(z), 128 * tile_of(z) + 128)
        x_ref[base : base + rows, lanes] = ref[z, :, 0:128]
        x_ref[base + rows : base + 2 * rows, lanes] = ref[z, :, 256:384]
    for pair in range(NZ // 2):
        lanes = slice(128 * tile_of_pair(pair), 128 * tile_of_pair(pair) + 128)
        even = ref[2 * pair, :, 128:256]
        odd = ref[2 * pair + 1, :, 128:256]
        x_ref[base : base + rows, lanes] = low_halves(even, odd)
        x_ref[base + rows : base + 2 * rows, lanes] = high_halves(even, odd)


def pack(ref, half, value, rows):
    for t in range(4):
        lanes = slice(128 * t, 128 * t + 128)
        ref[4 * half + t, :, 0:128] = value[:rows, lanes]
        ref[4 * half + t, :, 256:384] = value[rows:, lanes]
    for t in range(2):
        lanes = slice(512 + 128 * t, 640 + 128 * t)
        lower, upper = value[:rows, lanes], value[rows:, lanes]
        ref[4 * half + 2 * t, :, 128:256] = low_halves(lower, upper)
        ref[4 * half + 2 * t + 1, :, 128:256] = high_halves(lower, upper)


def bring(pairs, sems):
    copies = [
        pltpu.make_async_copy(source, target, sems.at[n]) for n, (source, target) in enumerate(pairs)
    ]
    for copy in copies:
        copy.start()
    return copies


def pack_kernel(points_hbm, wide_ref, send_ref, points_ref, sems):
    copies = bring([(points_hbm, points_ref)], sems)
    select = point_select()
    copies[0].wait()
    wide = dot_tn(points_ref[...], select).astype(BF)
    wide_ref[...] = wide
    for s in range(NZ):
        for first in range(2):
            send_ref[s, CB * first : CB * first + CB, :] = wide[
                CB * s : CB * s + CB, 384 * first : 384 * first + 384
            ]


def prepare_kernel(
    points_hbm,
    weights_hbm,
    real_hbm,
    imag_hbm,
    support_hbm,
    wide_ref,
    coupling_ref,
    masked_hbm,
    gain_ref,
    masked_ref,
    points_ref,
    weights_ref,
    real_ref,
    imag_ref,
    support_ref,
    sems,
):
    copies = bring(
        (
            (points_hbm, points_ref),
            (weights_hbm, weights_ref),
            (real_hbm, real_ref),
            (imag_hbm, imag_ref),
            (support_hbm, support_ref),
        ),
        sems,
    )
    select = point_select()
    copies[0].wait()
    wide_ref[...] = dot_tn(points_ref[...], select).astype(BF)

    for copy in copies[1:]:
        copy.wait()
    flip = lax.rem(lax.axis_index("lat"), 2) == 0
    lane = iota((1, 12), 1)
    seen = support_ref[...]
    seen = jnp.where(lane < 4, seen[:, 0:1], jnp.where(lane < 8, seen[:, 1:2], seen[:, 2:3]))
    seen = seen.astype(F32)
    rows = [weights_ref[k].astype(F32) for k in range(NK)]
    masked = jnp.concatenate([rows[k][i : i + 1] * seen for i in range(NR) for k in range(NK)], axis=0)
    turned = jnp.concatenate([masked[:, 8:12], masked[:, 4:8], masked[:, 0:4]], axis=1)
    masked = jnp.where(flip, turned, masked)
    masked_ref[...] = masked
    copies = bring([(masked_ref, masked_hbm)], sems)
    masked = masked.astype(BF)
    size = 12 * CB
    expand = (iota((size, 12), 0) // CB == iota((size, 12), 1)).astype(F32).astype(BF)
    same = (iota((size, size), 0) & 15) == (iota((size, size), 1) & 15)
    wide = dot_nt(dot(expand, masked).astype(BF), expand)
    coupling_ref[...] = jnp.where(same, wide, 0.0).astype(BF)

    lane = iota((MODES, 2 * MP), 1)
    odd = (lane >= MP).astype(jnp.int32)
    split = (iota((MODES, 2 * MP), 0) == 2 * (lane - MP * odd) + odd).astype(F32).astype(BF)
    first_half = jnp.where(iota((1, 2 * MP), 1) == 0, 0.5, 1.0).astype(F32)
    for part, ref in enumerate((real_ref, imag_ref)):
        rows = [ref[k] for k in range(NK)]
        rest = jnp.concatenate([rows[k][i : i + 1] for i in range(NR) for k in range(NK)], axis=0)
        moved = None
        for step in range(3):
            piece = rest.astype(BF)
            rest = rest - piece.astype(F32)
            term = dot(piece, split)
            moved = term if moved is None else moved + term
        gain_ref[12 * part : 12 * part + 12, :] = moved * first_half
    copies[0].wait()


def spectral(value, parity, table_ref, gain_ref, filt_ref, sign):
    spec = dot(value, table_ref[parity])
    lanes = slice(MP * parity, MP * parity + MP)
    for g in range(12):
        rows = slice(CB * g, CB * g + CB)
        part_a, part_b = spec[rows, :MP], spec[rows, MP:]
        real = gain_ref[g : g + 1, lanes]
        imag = sign * gain_ref[12 + g : 13 + g, lanes]
        filt_ref[parity, rows, :MP] = (real * part_a - imag * part_b).astype(BF)
        filt_ref[parity, rows, MP:] = (real * part_b + imag * part_a).astype(BF)


def transform(lower, upper, table_ref, gain_ref, filt_ref, sign, copies):
    for parity, value in enumerate((lower + upper, lower - upper)):
        copies[parity].wait()
        spectral(value.astype(BF), parity, table_ref, gain_ref, filt_ref, sign)
    even = dot_nt(filt_ref[0], table_ref[0])
    odd = dot_nt(filt_ref[1], table_ref[1])
    scale = 2.0 / NLON
    return ((even + odd) * scale).astype(BF), ((even - odd) * scale).astype(BF)


def filter_kernel(
    first_ref,
    own_ref,
    second_ref,
    coupling_ref,
    gain_ref,
    table_hbm,
    send_ref,
    x_ref,
    filt_ref,
    table_ref,
    sems,
):
    copies = bring([(table_hbm.at[p], table_ref.at[p]) for p in range(2)], sems)
    for band, ref in enumerate((first_ref, own_ref, second_ref)):
        unpack(ref, x_ref, 64 * band, 32)
    coupling = coupling_ref[...]
    lower = dot(coupling, x_ref[:, :KP])
    upper = dot(coupling, x_ref[:, KP:])
    lower, upper = transform(lower, upper, table_ref, gain_ref, filt_ref, 1.0, copies)
    pack(send_ref, 0, lower, 96)
    pack(send_ref, 1, upper, 96)


def gelu_parts(hidden):
    inner_part = GELU_SCALE * (hidden + CUBIC_TERM * hidden * hidden * hidden)
    tangent = jnp.tanh(inner_part)
    gelu_value = 0.5 * hidden * (1.0 + tangent)
    gelu_slope = 0.5 * (1.0 + tangent) + 0.5 * hidden * (1.0 - tangent * tangent) * GELU_SCALE * (
        1.0 + 3.0 * CUBIC_TERM * hidden * hidden
    )
    return (gelu_value, gelu_slope)


def mlp_kernel(
    recv_ref,
    fields_ref,
    cot_ref,
    filter_ref,
    inner_ref,
    outer_ref,
    back_hbm,
    grads_hbm,
    state_grad_hbm,
    back_ref,
    grads_ref,
    state_grad_ref,
    sems,
):
    mix = jnp.concatenate(
        [filter_ref[k, CB * s : CB * s + CB, :] for s in range(NZ) for k in range(NK)], axis=0
    )
    inner = inner_ref[...]
    outer = outer_ref[...]
    held = []
    for first in range(2):
        lanes = slice(384 * first, 384 * first + 384)
        filtered = jnp.concatenate(
            [recv_ref[s, 48 * first : 48 * first + 48, :] for s in range(NZ)], axis=0
        )
        cot = cot_ref[:, lanes]
        state = (fields_ref[:, lanes].astype(F32) + dot_tn(mix, filtered)).astype(BF)
        hidden = dot_tn(inner, state)
        value, slope = gelu_parts(hidden)
        active = value.astype(BF)
        d_hidden = (dot(outer, cot) * slope).astype(BF)
        d_state = cot.astype(F32) + dot(inner, d_hidden)
        state_grad_ref[:, lanes] = d_state
        d_state_b = d_state.astype(BF)
        back_ref[128 * first : 128 * first + 128, :] = d_state_b
        held.append((filtered, d_state_b, active, cot, state, d_hidden))
    copies = bring(((back_ref, back_hbm), (state_grad_ref, state_grad_hbm)), sems)
    sums = None
    for filtered, d_state_b, active, cot, state, d_hidden in held:
        parts = (dot_nt(filtered, d_state_b), dot_nt(active, cot), dot_nt(state, d_hidden))
        sums = parts if sums is None else tuple(a + b for a, b in zip(sums, parts))
    grads_ref[0:384, :] = sums[0].astype(BF)
    grads_ref[384:640, :] = sums[1].astype(BF)
    grads_ref[640:768, :] = sums[2][:, :128].astype(BF)
    grads_ref[768:896, :] = sums[2][:, 128:].astype(BF)
    grads_ref[896:WIDE, :] = jnp.zeros((WIDE - 896, 128), BF)
    last = pltpu.make_async_copy(grads_ref, grads_hbm, sems.at[2])
    last.start()
    for copy in copies + [last]:
        copy.wait()


def adjoint_kernel(
    recv_hbm,
    weights_ref,
    gain_ref,
    table_ref,
    filter_ref,
    first_ref,
    own_hbm,
    second_ref,
    x_ref,
    middle_ref,
    spec_ref,
    filt_ref,
    total_ref,
    own_ref,
    sems,
):
    pairs = []
    for n in range(NZ):
        lanes = pl.ds(128 * tile_of(n), 128)
        pairs.append((recv_hbm.at[n, :, pl.ds(0, 128)], x_ref.at[pl.ds(0, 256), lanes]))
        pairs.append((recv_hbm.at[n, :, pl.ds(256, 128)], x_ref.at[pl.ds(256, 256), lanes]))
        pairs.append((recv_hbm.at[n, :, pl.ds(128, 128)], middle_ref.at[n]))
    copies = bring(pairs, sems)
    z = lax.axis_index("lon")
    quarter = lax.rem(z, 4)
    sign = jnp.where(z < 4, 1.0, -1.0)
    main = pl.ds(pl.multiple_of(128 * quarter, 128), 128)
    tail = pl.ds(pl.multiple_of(512 + 64 * quarter, 64), 64)
    places = [
        jnp.concatenate([table_ref[p, main, :], table_ref[p, tail, :]], axis=0) for p in range(2)
    ]
    for copy in copies:
        copy.wait()
    for pair in range(NZ // 2):
        lanes = slice(128 * tile_of_pair(pair), 128 * tile_of_pair(pair) + 128)
        even, odd = middle_ref[2 * pair], middle_ref[2 * pair + 1]
        x_ref[0:256, lanes] = low_halves(even, odd)
        x_ref[256:512, lanes] = high_halves(even, odd)
    for i in range(NR):
        rows = slice(128 * i, 128 * i + 128)
        lower = x_ref[rows, :KP].astype(F32)
        upper = x_ref[rows, KP:].astype(F32)
        spec_ref[0, rows, :] = dot((lower + upper).astype(BF), table_ref[0])
        spec_ref[1, rows, :] = dot((lower - upper).astype(BF), table_ref[1])
    for i in range(NR):
        rows = slice(128 * i, 128 * i + 128)
        for parity in range(2):
            lanes = slice(MP * parity, MP * parity + MP)
            part_a, part_b = spec_ref[parity, rows, :MP], spec_ref[parity, rows, MP:]
            for k in range(NK):
                g = NK * i + k
                real = gain_ref[g : g + 1, lanes]
                imag = gain_ref[12 + g : 13 + g, lanes]
                block = slice(128 * k, 128 * k + 128)
                filt_ref[i, parity, block, :MP] = (real * part_a + imag * part_b).astype(BF)
                filt_ref[i, parity, block, MP:] = (real * part_b - imag * part_a).astype(BF)
        result = dot_nt(filt_ref[i, 0], places[0]) + sign * dot_nt(filt_ref[i, 1], places[1])
        result = (result * (2.0 / NLON)).astype(BF)
        parts = [dot(filter_ref[k], result[128 * k : 128 * k + 128]) for k in range(NK)]
        for q in range(12):
            total = weights_ref[NK * i, q] * parts[0]
            for k in range(1, NK):
                total = total + weights_ref[NK * i + k, q] * parts[k]
            total_ref[q] = total if i == 0 else total_ref[q] + total
    for band, ref in enumerate((first_ref, own_ref, second_ref)):
        for first in range(2):
            lower, upper = total_ref[4 * band + first], total_ref[4 * band + 2 + first]
            base = 384 * first
            dtype = ref.dtype
            ref[:, base : base + 128] = lower[:, :128].astype(dtype)
            middle = jnp.concatenate([lower[:, 128:], upper[:, 128:]], axis=1)
            ref[:, base + 128 : base + 256] = middle.astype(dtype)
            ref[:, base + 256 : base + 384] = upper[:, :128].astype(dtype)
    bring([(own_ref, own_hbm)], sems)[0].wait()


def sum_kernel(copies, recv_ref, out_ref):
    total = recv_ref[0].astype(F32)
    for n in range(1, recv_ref.shape[0]):
        total = total + recv_ref[n].astype(F32)
    total = total.astype(BF)
    for n in range(copies):
        out_ref[n] = total


def field_kernel(own_hbm, state_grad_hbm, first_ref, second_ref, grad_ref, own_ref, state_grad_ref, sems):
    copies = bring(((own_hbm, own_ref), (state_grad_hbm, state_grad_ref)), sems)
    select = point_select()
    for copy in copies:
        copy.wait()
    lat_part = own_ref[...] + first_ref[...].astype(F32) + second_ref[...].astype(F32)
    total = state_grad_ref[...] + lat_part.astype(BF).astype(F32)
    grad_ref[...] = dot_nt(select, total.astype(BF)).astype(BF)


def weights_kernel(scale, grads_ref, filter_ref, inner_ref, outer_ref):
    for s in range(NZ):
        for k in range(NK):
            base = 48 * s + CB * k
            filter_ref[k, CB * s : CB * s + CB, :] = grads_ref[base : base + CB, :].astype(F32) * scale
    outer_ref[...] = grads_ref[384:640, :].astype(F32) * scale
    inner_ref[:, :128] = grads_ref[640:768, :].astype(F32) * scale
    inner_ref[:, 128:] = grads_ref[768:896, :].astype(F32) * scale


def call(kernel, outs, flops, scratch=(), in_specs=None, out_specs=None):
    shapes = outs if isinstance(outs, tuple) else (outs,)
    moved = sum(math.prod(o.shape) * o.dtype.itemsize for o in shapes)
    if out_specs is None:
        out_specs = jax.tree.map(lambda _: pl.BlockSpec(memory_space=pltpu.VMEM), outs)
    return pl.pallas_call(
        kernel,
        out_shape=outs,
        in_specs=in_specs,
        out_specs=out_specs,
        scratch_shapes=scratch,
        compiler_params=pltpu.CompilerParams(vmem_limit_bytes=LIMIT),
        cost_estimate=pl.CostEstimate(flops=flops, bytes_accessed=2 * moved, transcendentals=0),
    )


def shaped(shape, dtype=BF):
    return jax.ShapeDtypeStruct(shape, dtype)


def in_hbm(shape, dtype=BF):
    return pltpu.HBM(shape, dtype)


def hold(value):
    return pltpu.with_memory_space_constraint(value, pltpu.HBM)


def vmem(count):
    return [pl.BlockSpec(memory_space=pltpu.VMEM)] * count


def hbm(count):
    return [pl.BlockSpec(memory_space=pltpu.HBM)] * count


def swapped(value, first):
    count = lax.axis_size("lat")
    pairs = []
    for low in range(first, count - 1, 2):
        pairs += [(low, low + 1), (low + 1, low)]
    return lax.ppermute(value, "lat", pairs)


def local(
    fields,
    cotangent,
    basis_weights,
    band_support,
    spectrum_real,
    spectrum_imag,
    filter_weights,
    inner_weights,
    outer_weights,
):
    group = lax.axis_size("ens") * lax.axis_size("lat")
    grad_scale = 1.0 / math.sqrt(group * NR * NLON)
    table = jnp.asarray(dft_table())

    field_points = fields[0].transpose(1, 0, 2).reshape(LON * NR, 128)
    cot_points = cotangent[0].transpose(1, 0, 2).reshape(LON * NR, 128)
    field_wide, send_fields = call(
        pack_kernel, (shaped((128, 768)), shaped((NZ, 32, 384))), 2 * 720 * 768 * 128,
        [pltpu.VMEM((720, 128), BF), pltpu.SemaphoreType.DMA((1,))], hbm(1)
    )(hold(field_points))
    own = lax.all_to_all(send_fields, "lon", 0, 0, tiled=True)

    cot_wide, coupling, masked, gains = call(
        prepare_kernel,
        (
            shaped((128, 768)),
            shaped((192, 192)),
            in_hbm((12, 12), F32),
            shaped((24, 2 * MP), F32),
        ),
        2 * 720 * 768 * 128,
        [
            pltpu.VMEM((12, 12), F32),
            pltpu.VMEM((720, 128), BF),
            pltpu.VMEM((NK, NR, 12), BF),
            pltpu.VMEM((NK, NR, MODES), F32),
            pltpu.VMEM((NK, NR, MODES), F32),
            pltpu.VMEM((1, 3), jnp.int32),
            pltpu.SemaphoreType.DMA((5,)),
        ],
        hbm(5),
        tuple(vmem(2) + hbm(1) + vmem(1)),
    )(
        hold(cot_points),
        hold(basis_weights),
        hold(spectrum_real),
        hold(spectrum_imag),
        hold(band_support),
    )

    first = swapped(own, 0)
    second = swapped(own, 1)
    work = [
        pltpu.VMEM((192, 2 * KP), BF),
        pltpu.VMEM((2, 192, 2 * MP), BF),
        pltpu.VMEM((2, KP, 2 * MP), BF),
        pltpu.SemaphoreType.DMA((3,)),
    ]
    send_filtered = call(
        filter_kernel, shaped((NZ, 96, 384)), 8 * 192 * KP * KP, work, vmem(5) + hbm(1)
    )(first, own, second, coupling, gains, hold(table))
    filtered = lax.all_to_all(send_filtered, "lon", 0, 0, tiled=True)

    back, grads, state_grad = call(
        mlp_kernel,
        (in_hbm((256, 384)), in_hbm((WIDE, 128)), in_hbm((128, 768), F32)),
        2 * 768 * 128 * 256 * 10,
        [
            pltpu.VMEM((256, 384), BF),
            pltpu.VMEM((WIDE, 128), BF),
            pltpu.VMEM((128, 768), F32),
            pltpu.SemaphoreType.DMA((3,)),
        ],
        vmem(6),
        tuple(hbm(3)),
    )(filtered, field_wide, cot_wide, filter_weights, inner_weights, outer_weights)
    back = lax.all_gather(back, "lon", tiled=True).reshape(NZ, 256, 384)

    def summed(value, copies):
        return call(
            functools.partial(sum_kernel, copies),
            shaped((copies,) + value.shape[1:]),
            value.size,
            (),
            vmem(1),
        )(value)

    share = WIDE // group
    chunks = lax.all_to_all(grads.reshape(group, share, 128), ("ens", "lat"), 0, 0, tiled=True)
    chunks = lax.all_to_all(summed(chunks, NZ), "lon", 0, 0, tiled=True)
    gathered = lax.all_to_all(summed(chunks, group), ("ens", "lat"), 0, 0, tiled=True)

    to_first, kept, to_second = call(
        adjoint_kernel,
        (shaped((128, 768)), in_hbm((128, 768), F32), shaped((128, 768))),
        4 * 512 * KP * KP + 4 * 1536 * KP * 192,
        [
            pltpu.VMEM((512, 2 * KP), BF),
            pltpu.VMEM((NZ, 256, 128), BF),
            pltpu.VMEM((2, 512, 2 * MP), F32),
            pltpu.VMEM((NR, 2, 384, 2 * MP), BF),
            pltpu.VMEM((12, 128, 192), F32),
            pltpu.VMEM((128, 768), F32),
            pltpu.SemaphoreType.DMA((3 * NZ,)),
        ],
        hbm(1) + [pl.BlockSpec(memory_space=pltpu.SMEM)] + vmem(3),
        tuple(vmem(1) + hbm(1) + vmem(1)),
    )(hold(back), masked, gains, table, filter_weights)
    from_first = swapped(to_first, 0)
    from_second = swapped(to_second, 1)
    grad_points = call(
        field_kernel,
        shaped((LON * NR, 128)),
        2 * 720 * 768 * 128,
        [
            pltpu.VMEM((128, 768), F32),
            pltpu.VMEM((128, 768), F32),
            pltpu.SemaphoreType.DMA((2,)),
        ],
        hbm(2) + vmem(2),
    )(hold(kept), hold(state_grad), from_first, from_second)

    filter_grad, inner_grad, outer_grad = call(
        functools.partial(weights_kernel, grad_scale),
        (shaped((NK, 128, 128), F32), shaped((128, 256), F32), shaped((256, 128), F32)),
        WIDE * 128,
        (),
        vmem(1),
    )(gathered.reshape(WIDE, 128))
    field_grad = grad_points.reshape(LON, NR, 128).transpose(1, 0, 2)[None]
    return (field_grad, filter_grad, inner_grad, outer_grad)


def solution(mesh):
    placed = (
        P("ens", "lat", "lon", None),
        P("ens", "lat", "lon", None),
        P(None, "lat", None),
        P("lat", None),
        P(None, "lat", None),
        P(None, "lat", None),
        P(),
        P(),
        P(),
    )
    return jax.shard_map(
        local,
        mesh=mesh,
        in_specs=placed,
        out_specs=(P("ens", "lat", "lon", None), P(), P(), P()),
        check_vma=False,
    )
```

```python
import functools
import math

import jax
import jax.numpy as jnp
import ml_dtypes
import numpy as np
from jax import lax
from jax.experimental import pallas as pl
from jax.experimental.pallas import tpu as pltpu
from jax.sharding import PartitionSpec as P

GELU_SCALE = 0.7978845608028654
CUBIC_TERM = 0.044715
BF = jnp.bfloat16
F32 = jnp.float32
NLON = 1440
NZ = 8
LON = 180
MODES = 720
MP = 384
KP = 768
CB = 16
NK = 3
NR = 4
WIDE = 1024
LIMIT = 24 * 1024 * 1024


def dft_table():
    lane = np.arange(KP)
    tail = lane >= 512
    owner = np.where(tail, 2 * ((lane - 512) // 128) + (lane % 128 >= 64), lane // 128)
    place = np.where(tail, 128 + lane % 64, lane % 128)
    column = owner * LON + place
    tables = []
    for parity in range(2):
        frequency = 2 * np.arange(MP) + parity
        phase = 2.0 * math.pi * ((column[:, None] * frequency[None, :]) % NLON) / NLON
        valid = (place < LON)[:, None] & (frequency < MODES)[None, :]
        cos = np.where(valid, np.cos(phase), 0.0)
        sin = np.where(valid, -np.sin(phase), 0.0)
        tables.append(np.concatenate([cos, sin], axis=1))
    return np.stack(tables).astype(ml_dtypes.bfloat16)


def dot(a, b):
    return jnp.dot(a, b, preferred_element_type=F32)


def dot_tn(a, b):
    return lax.dot_general(a, b, (((0,), (0,)), ((), ())), preferred_element_type=F32)


def dot_nt(a, b):
    return lax.dot_general(a, b, (((1,), (1,)), ((), ())), preferred_element_type=F32)


def low_halves(a, b):
    return jnp.concatenate([a[:, :64], b[:, :64]], axis=1)


def high_halves(a, b):
    return jnp.concatenate([a[:, 64:], b[:, 64:]], axis=1)


def iota(shape, dim):
    return lax.broadcasted_iota(jnp.int32, shape, dim)


def point_select():
    lane = iota((8, 2 * 384), 1)
    first = (lane >= 384).astype(jnp.int32)
    lane = lane - 384 * first
    middle = (lane >= 128) & (lane < 256)
    upper = ((lane >= 192)).astype(jnp.int32)
    place = jnp.where(middle, 128 + (lane & 63), lane & 127)
    point = jnp.where(place < LON, place * NR + 2 * upper + first, -1)
    return (iota((LON * NR, 2 * 384), 0) == point[0:1]).astype(F32).astype(BF)


def tile_of(z):
    return 6 * (z // 4) + z % 4


def tile_of_pair(pair):
    return 6 * (pair // 2) + 4 + pair % 2


def unpack(ref, x_ref, base, rows):
    for z in range(NZ):
        lanes = slice(128 * tile_of(z), 128 * tile_of(z) + 128)
        x_ref[base : base + rows, lanes] = ref[z, :, 0:128]
        x_ref[base + rows : base + 2 * rows, lanes] = ref[z, :, 256:384]
    for pair in range(NZ // 2):
        lanes = slice(128 * tile_of_pair(pair), 128 * tile_of_pair(pair) + 128)
        even = ref[2 * pair, :, 128:256]
        odd = ref[2 * pair + 1, :, 128:256]
        x_ref[base : base + rows, lanes] = low_halves(even, odd)
        x_ref[base + rows : base + 2 * rows, lanes] = high_halves(even, odd)


def pack(ref, half, value, rows):
    for t in range(4):
        lanes = slice(128 * t, 128 * t + 128)
        ref[4 * half + t, :, 0:128] = value[:rows, lanes]
        ref[4 * half + t, :, 256:384] = value[rows:, lanes]
    for t in range(2):
        lanes = slice(512 + 128 * t, 640 + 128 * t)
        lower, upper = value[:rows, lanes], value[rows:, lanes]
        ref[4 * half + 2 * t, :, 128:256] = low_halves(lower, upper)
        ref[4 * half + 2 * t + 1, :, 128:256] = high_halves(lower, upper)


def bring(pairs, sems):
    copies = [
        pltpu.make_async_copy(source, target, sems.at[n]) for n, (source, target) in enumerate(pairs)
    ]
    for copy in copies:
        copy.start()
    return copies


def pack_kernel(points_hbm, wide_ref, send_ref, points_ref, sems):
    copies = bring([(points_hbm, points_ref)], sems)
    select = point_select()
    copies[0].wait()
    wide = dot_tn(points_ref[...], select).astype(BF)
    wide_ref[...] = wide
    for s in range(NZ):
        for first in range(2):
            send_ref[s, CB * first : CB * first + CB, :] = wide[
                CB * s : CB * s + CB, 384 * first : 384 * first + 384
            ]


def prepare_kernel(
    points_hbm,
    weights_hbm,
    real_hbm,
    imag_hbm,
    support_hbm,
    wide_ref,
    coupling_ref,
    turned_hbm,
    gain_ref,
    turned_ref,
    points_ref,
    weights_ref,
    real_ref,
    imag_ref,
    support_ref,
    sems,
):
    copies = bring(
        (
            (points_hbm, points_ref),
            (weights_hbm, weights_ref),
            (real_hbm, real_ref),
            (imag_hbm, imag_ref),
            (support_hbm, support_ref),
        ),
        sems,
    )
    select = point_select()
    copies[0].wait()
    wide_ref[...] = dot_tn(points_ref[...], select).astype(BF)

    for copy in copies[1:]:
        copy.wait()
    flip = lax.rem(lax.axis_index("lat"), 2) == 0
    lane = iota((1, 12), 1)
    seen = support_ref[...]
    seen = jnp.where(lane < 4, seen[:, 0:1], jnp.where(lane < 8, seen[:, 1:2], seen[:, 2:3]))
    seen = seen.astype(F32)
    rows = [weights_ref[k].astype(F32) for k in range(NK)]
    masked = jnp.concatenate([rows[k][i : i + 1] * seen for i in range(NR) for k in range(NK)], axis=0)
    turned = jnp.concatenate([masked[:, 8:12], masked[:, 4:8], masked[:, 0:4]], axis=1)
    masked = jnp.where(flip, turned, masked).astype(BF)
    size = 12 * CB
    expand = (iota((size, 12), 0) // CB == iota((size, 12), 1)).astype(F32).astype(BF)
    same = (iota((size, size), 0) & 15) == (iota((size, size), 1) & 15)
    wide = dot_nt(dot(expand, masked).astype(BF), expand)
    coupling_ref[...] = jnp.where(same, wide, 0.0).astype(BF)
    wide = dot_nt(dot_nt(expand, masked).astype(BF), expand)
    turned_ref[...] = jnp.where(same, wide, 0.0).astype(BF)
    copies = bring([(turned_ref, turned_hbm)], sems)

    lane = iota((MODES, 2 * MP), 1)
    odd = (lane >= MP).astype(jnp.int32)
    split = (iota((MODES, 2 * MP), 0) == 2 * (lane - MP * odd) + odd).astype(F32).astype(BF)
    first_half = jnp.where(iota((1, 2 * MP), 1) == 0, 0.5, 1.0).astype(F32)
    for part, ref in enumerate((real_ref, imag_ref)):
        rows = [ref[k] for k in range(NK)]
        rest = jnp.concatenate([rows[k][i : i + 1] for i in range(NR) for k in range(NK)], axis=0)
        moved = None
        for step in range(3):
            piece = rest.astype(BF)
            rest = rest - piece.astype(F32)
            term = dot(piece, split)
            moved = term if moved is None else moved + term
        gain_ref[12 * part : 12 * part + 12, :] = moved * first_half
    copies[0].wait()


def spectral(value, parity, table_ref, gain_ref, filt_ref, sign):
    spec = dot(value, table_ref[parity])
    lanes = slice(MP * parity, MP * parity + MP)
    for g in range(12):
        rows = slice(CB * g, CB * g + CB)
        part_a, part_b = spec[rows, :MP], spec[rows, MP:]
        real = gain_ref[g : g + 1, lanes]
        imag = sign * gain_ref[12 + g : 13 + g, lanes]
        filt_ref[parity, rows, :MP] = (real * part_a - imag * part_b).astype(BF)
        filt_ref[parity, rows, MP:] = (real * part_b + imag * part_a).astype(BF)


def transform(lower, upper, table_ref, gain_ref, filt_ref, sign, copies):
    for parity, value in enumerate((lower + upper, lower - upper)):
        copies[parity].wait()
        spectral(value.astype(BF), parity, table_ref, gain_ref, filt_ref, sign)
    even = dot_nt(filt_ref[0], table_ref[0])
    odd = dot_nt(filt_ref[1], table_ref[1])
    scale = 2.0 / NLON
    return ((even + odd) * scale).astype(BF), ((even - odd) * scale).astype(BF)


def filter_kernel(
    first_ref,
    own_ref,
    second_ref,
    coupling_ref,
    gain_ref,
    table_hbm,
    send_ref,
    x_ref,
    filt_ref,
    table_ref,
    sems,
):
    copies = bring([(table_hbm.at[p], table_ref.at[p]) for p in range(2)], sems)
    for band, ref in enumerate((first_ref, own_ref, second_ref)):
        unpack(ref, x_ref, 64 * band, 32)
    coupling = coupling_ref[...]
    lower = dot(coupling, x_ref[:, :KP])
    upper = dot(coupling, x_ref[:, KP:])
    lower, upper = transform(lower, upper, table_ref, gain_ref, filt_ref, 1.0, copies)
    pack(send_ref, 0, lower, 96)
    pack(send_ref, 1, upper, 96)


def gelu_parts(hidden):
    inner_part = GELU_SCALE * (hidden + CUBIC_TERM * hidden * hidden * hidden)
    tangent = jnp.tanh(inner_part)
    gelu_value = 0.5 * hidden * (1.0 + tangent)
    gelu_slope = 0.5 * (1.0 + tangent) + 0.5 * hidden * (1.0 - tangent * tangent) * GELU_SCALE * (
        1.0 + 3.0 * CUBIC_TERM * hidden * hidden
    )
    return (gelu_value, gelu_slope)


def mlp_kernel(
    recv_ref,
    fields_ref,
    cot_ref,
    filter_ref,
    inner_ref,
    outer_ref,
    back_hbm,
    grads_hbm,
    state_grad_hbm,
    back_ref,
    grads_ref,
    state_grad_ref,
    sems,
):
    mix = jnp.concatenate(
        [filter_ref[k, CB * s : CB * s + CB, :] for s in range(NZ) for k in range(NK)], axis=0
    )
    inner = inner_ref[...]
    outer = outer_ref[...]
    held = []
    for first in range(2):
        lanes = slice(384 * first, 384 * first + 384)
        filtered = jnp.concatenate(
            [recv_ref[s, 48 * first : 48 * first + 48, :] for s in range(NZ)], axis=0
        )
        cot = cot_ref[:, lanes]
        state = (fields_ref[:, lanes].astype(F32) + dot_tn(mix, filtered)).astype(BF)
        hidden = dot_tn(inner, state)
        value, slope = gelu_parts(hidden)
        active = value.astype(BF)
        d_hidden = (dot(outer, cot) * slope).astype(BF)
        d_state = cot.astype(F32) + dot(inner, d_hidden)
        state_grad_ref[:, lanes] = d_state
        d_state_b = d_state.astype(BF)
        back_ref[128 * first : 128 * first + 128, :] = d_state_b
        held.append((filtered, d_state_b, active, cot, state, d_hidden))
    copies = bring(((back_ref, back_hbm), (state_grad_ref, state_grad_hbm)), sems)
    sums = None
    for filtered, d_state_b, active, cot, state, d_hidden in held:
        parts = (dot_nt(filtered, d_state_b), dot_nt(active, cot), dot_nt(state, d_hidden))
        sums = parts if sums is None else tuple(a + b for a, b in zip(sums, parts))
    grads_ref[0:384, :] = sums[0].astype(BF)
    grads_ref[384:640, :] = sums[1].astype(BF)
    grads_ref[640:768, :] = sums[2][:, :128].astype(BF)
    grads_ref[768:896, :] = sums[2][:, 128:].astype(BF)
    grads_ref[896:WIDE, :] = jnp.zeros((WIDE - 896, 128), BF)
    last = pltpu.make_async_copy(grads_ref, grads_hbm, sems.at[2])
    last.start()
    for copy in copies + [last]:
        copy.wait()


def adjoint_kernel(
    recv_hbm,
    turned_hbm,
    state_grad_hbm,
    gain_ref,
    table_ref,
    filter_ref,
    first_ref,
    base_hbm,
    second_ref,
    x_ref,
    middle_ref,
    spec_ref,
    filt_ref,
    part_ref,
    turned_ref,
    state_grad_ref,
    base_ref,
    sems,
):
    pairs = [(recv_hbm.at[n, :, pl.ds(128, 128)], middle_ref.at[n]) for n in range(NZ)]
    for half in range(2):
        for n in range(NZ):
            lanes = pl.ds(128 * tile_of(n), 128)
            rows = pl.ds(256 * half, 256)
            pairs.append((recv_hbm.at[n, :, pl.ds(256 * half, 128)], x_ref.at[rows, lanes]))
    pairs += [(turned_hbm, turned_ref), (state_grad_hbm, state_grad_ref)]
    copies = bring(pairs, sems)
    z = lax.axis_index("lon")
    quarter = lax.rem(z, 4)
    sign = jnp.where(z < 4, 1.0, -1.0)
    main = pl.ds(pl.multiple_of(128 * quarter, 128), 128)
    tail = pl.ds(pl.multiple_of(512 + 64 * quarter, 64), 64)
    places = [
        jnp.concatenate([table_ref[p, main, :], table_ref[p, tail, :]], axis=0) for p in range(2)
    ]
    for half in range(2):
        for copy in copies[0 : 2 * NZ] if half == 0 else copies[2 * NZ :]:
            copy.wait()
        block = slice(256 * half, 256 * half + 256)
        for pair in range(NZ // 2):
            lanes = slice(128 * tile_of_pair(pair), 128 * tile_of_pair(pair) + 128)
            even, odd = middle_ref[2 * pair], middle_ref[2 * pair + 1]
            x_ref[block, lanes] = low_halves(even, odd) if half == 0 else high_halves(even, odd)
        lower = x_ref[block, :KP].astype(F32)
        upper = x_ref[block, KP:].astype(F32)
        spec_ref[0, block, :] = dot((lower + upper).astype(BF), table_ref[0])
        spec_ref[1, block, :] = dot((lower - upper).astype(BF), table_ref[1])
        for i in (2 * half, 2 * half + 1):
            rows = slice(128 * i, 128 * i + 128)
            for parity in range(2):
                lanes = slice(MP * parity, MP * parity + MP)
                part_a, part_b = spec_ref[parity, rows, :MP], spec_ref[parity, rows, MP:]
                for k in range(NK):
                    g = NK * i + k
                    real = gain_ref[g : g + 1, lanes]
                    imag = gain_ref[12 + g : 13 + g, lanes]
                    out = slice(128 * k, 128 * k + 128)
                    filt_ref[i, parity, out, :MP] = (real * part_a + imag * part_b).astype(BF)
                    filt_ref[i, parity, out, MP:] = (real * part_b - imag * part_a).astype(BF)
            result = dot_nt(filt_ref[i, 0], places[0]) + sign * dot_nt(filt_ref[i, 1], places[1])
            result = (result * (2.0 / NLON)).astype(BF)
            for k in range(NK):
                part = dot(filter_ref[k], result[128 * k : 128 * k + 128])
                part_ref[NK * i + k] = part.astype(BF)
    for s in range(NZ):
        rows = slice(CB * s, CB * s + CB)
        parts = jnp.concatenate([part_ref[g, rows, :] for g in range(12)], axis=0)
        total = dot(turned_ref[...], parts)
        for band, ref in enumerate((first_ref, base_ref, second_ref)):
            for first in range(2):
                base = 64 * band + CB * first
                lower, upper = total[base : base + CB], total[base + 32 : base + 32 + CB]
                middle = jnp.concatenate([lower[:, 128:], upper[:, 128:]], axis=1)
                for tile, value in enumerate((lower[:, :128], middle, upper[:, :128])):
                    lanes = slice(384 * first + 128 * tile, 384 * first + 128 * tile + 128)
                    if band == 1:
                        ref[rows, lanes] = value + state_grad_ref[rows, lanes]
                    else:
                        ref[rows, lanes] = value.astype(BF)
    bring([(base_ref, base_hbm)], sems)[0].wait()


def sum_kernel(copies, recv_ref, out_ref):
    total = recv_ref[0].astype(F32)
    for n in range(1, recv_ref.shape[0]):
        total = total + recv_ref[n].astype(F32)
    total = total.astype(BF)
    for n in range(copies):
        out_ref[n] = total


def field_kernel(base_hbm, first_ref, second_ref, grad_ref, base_ref, sems):
    copies = bring([(base_hbm, base_ref)], sems)
    select = point_select()
    halo = first_ref[...].astype(F32) + second_ref[...].astype(F32)
    copies[0].wait()
    grad_ref[...] = dot_nt(select, (base_ref[...] + halo).astype(BF)).astype(BF)


def weights_kernel(scale, grads_ref, filter_ref, inner_ref, outer_ref):
    for s in range(NZ):
        for k in range(NK):
            base = 48 * s + CB * k
            filter_ref[k, CB * s : CB * s + CB, :] = grads_ref[base : base + CB, :].astype(F32) * scale
    outer_ref[...] = grads_ref[384:640, :].astype(F32) * scale
    inner_ref[:, :128] = grads_ref[640:768, :].astype(F32) * scale
    inner_ref[:, 128:] = grads_ref[768:896, :].astype(F32) * scale


def call(kernel, outs, flops, scratch=(), in_specs=None, out_specs=None):
    shapes = outs if isinstance(outs, tuple) else (outs,)
    moved = sum(math.prod(o.shape) * o.dtype.itemsize for o in shapes)
    if out_specs is None:
        out_specs = jax.tree.map(lambda _: pl.BlockSpec(memory_space=pltpu.VMEM), outs)
    return pl.pallas_call(
        kernel,
        out_shape=outs,
        in_specs=in_specs,
        out_specs=out_specs,
        scratch_shapes=scratch,
        compiler_params=pltpu.CompilerParams(vmem_limit_bytes=LIMIT),
        cost_estimate=pl.CostEstimate(flops=flops, bytes_accessed=2 * moved, transcendentals=0),
    )


def shaped(shape, dtype=BF):
    return jax.ShapeDtypeStruct(shape, dtype)


def in_hbm(shape, dtype=BF):
    return pltpu.HBM(shape, dtype)


def hold(value):
    return pltpu.with_memory_space_constraint(value, pltpu.HBM)


def vmem(count):
    return [pl.BlockSpec(memory_space=pltpu.VMEM)] * count


def hbm(count):
    return [pl.BlockSpec(memory_space=pltpu.HBM)] * count


def swapped(value, first):
    count = lax.axis_size("lat")
    pairs = []
    for low in range(first, count - 1, 2):
        pairs += [(low, low + 1), (low + 1, low)]
    return lax.ppermute(value, "lat", pairs)


def local(
    fields,
    cotangent,
    basis_weights,
    band_support,
    spectrum_real,
    spectrum_imag,
    filter_weights,
    inner_weights,
    outer_weights,
):
    group = lax.axis_size("ens") * lax.axis_size("lat")
    grad_scale = 1.0 / math.sqrt(group * NR * NLON)
    table = jnp.asarray(dft_table())

    field_points = fields[0].transpose(1, 0, 2).reshape(LON * NR, 128)
    cot_points = cotangent[0].transpose(1, 0, 2).reshape(LON * NR, 128)
    field_wide, send_fields = call(
        pack_kernel, (shaped((128, 768)), shaped((NZ, 32, 384))), 2 * 720 * 768 * 128,
        [pltpu.VMEM((720, 128), BF), pltpu.SemaphoreType.DMA((1,))], hbm(1)
    )(hold(field_points))
    own = lax.all_to_all(send_fields, "lon", 0, 0, tiled=True)

    cot_wide, coupling, turned, gains = call(
        prepare_kernel,
        (
            shaped((128, 768)),
            shaped((192, 192)),
            in_hbm((192, 192)),
            shaped((24, 2 * MP), F32),
        ),
        2 * 720 * 768 * 128,
        [
            pltpu.VMEM((192, 192), BF),
            pltpu.VMEM((720, 128), BF),
            pltpu.VMEM((NK, NR, 12), BF),
            pltpu.VMEM((NK, NR, MODES), F32),
            pltpu.VMEM((NK, NR, MODES), F32),
            pltpu.VMEM((1, 3), jnp.int32),
            pltpu.SemaphoreType.DMA((5,)),
        ],
        hbm(5),
        tuple(vmem(2) + hbm(1) + vmem(1)),
    )(
        hold(cot_points),
        hold(basis_weights),
        hold(spectrum_real),
        hold(spectrum_imag),
        hold(band_support),
    )

    first = swapped(own, 0)
    second = swapped(own, 1)
    work = [
        pltpu.VMEM((192, 2 * KP), BF),
        pltpu.VMEM((2, 192, 2 * MP), BF),
        pltpu.VMEM((2, KP, 2 * MP), BF),
        pltpu.SemaphoreType.DMA((3,)),
    ]
    send_filtered = call(
        filter_kernel, shaped((NZ, 96, 384)), 8 * 192 * KP * KP, work, vmem(5) + hbm(1)
    )(first, own, second, coupling, gains, hold(table))
    filtered = lax.all_to_all(send_filtered, "lon", 0, 0, tiled=True)

    back, grads, state_grad = call(
        mlp_kernel,
        (in_hbm((256, 384)), in_hbm((WIDE, 128)), in_hbm((128, 768), F32)),
        2 * 768 * 128 * 256 * 10,
        [
            pltpu.VMEM((256, 384), BF),
            pltpu.VMEM((WIDE, 128), BF),
            pltpu.VMEM((128, 768), F32),
            pltpu.SemaphoreType.DMA((3,)),
        ],
        vmem(6),
        tuple(hbm(3)),
    )(filtered, field_wide, cot_wide, filter_weights, inner_weights, outer_weights)
    back = lax.all_gather(back, "lon", tiled=True).reshape(NZ, 256, 384)

    def summed(value, copies):
        return call(
            functools.partial(sum_kernel, copies),
            shaped((copies,) + value.shape[1:]),
            value.size,
            (),
            vmem(1),
        )(value)

    share = WIDE // group
    chunks = lax.all_to_all(grads.reshape(group, share, 128), ("ens", "lat"), 0, 0, tiled=True)
    chunks = lax.all_to_all(summed(chunks, NZ), "lon", 0, 0, tiled=True)
    gathered = lax.all_to_all(summed(chunks, group), ("ens", "lat"), 0, 0, tiled=True)

    to_first, kept, to_second = call(
        adjoint_kernel,
        (shaped((128, 768)), in_hbm((128, 768), F32), shaped((128, 768))),
        4 * 512 * KP * KP + 4 * 1536 * KP * 192,
        [
            pltpu.VMEM((512, 2 * KP), BF),
            pltpu.VMEM((NZ, 256, 128), BF),
            pltpu.VMEM((2, 512, 2 * MP), F32),
            pltpu.VMEM((NR, 2, 384, 2 * MP), BF),
            pltpu.VMEM((12, 128, 192), BF),
            pltpu.VMEM((192, 192), BF),
            pltpu.VMEM((128, 768), F32),
            pltpu.VMEM((128, 768), F32),
            pltpu.SemaphoreType.DMA((3 * NZ + 2,)),
        ],
        hbm(3) + vmem(3),
        tuple(vmem(1) + hbm(1) + vmem(1)),
    )(hold(back), hold(turned), hold(state_grad), gains, table, filter_weights)
    from_second = swapped(to_second, 1)
    from_first = swapped(to_first, 0)
    grad_points = call(
        field_kernel,
        shaped((LON * NR, 128)),
        2 * 720 * 768 * 128,
        [pltpu.VMEM((128, 768), F32), pltpu.SemaphoreType.DMA((1,))],
        hbm(1) + vmem(2),
    )(hold(kept), from_second, from_first)

    filter_grad, inner_grad, outer_grad = call(
        functools.partial(weights_kernel, grad_scale),
        (shaped((NK, 128, 128), F32), shaped((128, 256), F32), shaped((256, 128), F32)),
        WIDE * 128,
        (),
        vmem(1),
    )(gathered.reshape(WIDE, 128))
    field_grad = grad_points.reshape(LON, NR, 128).transpose(1, 0, 2)[None]
    return (field_grad, filter_grad, inner_grad, outer_grad)


def solution(mesh):
    placed = (
        P("ens", "lat", "lon", None),
        P("ens", "lat", "lon", None),
        P(None, "lat", None),
        P("lat", None),
        P(None, "lat", None),
        P(None, "lat", None),
        P(),
        P(),
        P(),
    )
    return jax.shard_map(
        local,
        mesh=mesh,
        in_specs=placed,
        out_specs=(P("ens", "lat", "lon", None), P(), P(), P()),
        check_vma=False,
    )
```

```python
import functools
import math

import jax
import jax.numpy as jnp
import ml_dtypes
import numpy as np
from jax import lax
from jax.experimental import pallas as pl
from jax.experimental.pallas import tpu as pltpu
from jax.sharding import PartitionSpec as P

GELU_SCALE = 0.7978845608028654
CUBIC_TERM = 0.044715
BF = jnp.bfloat16
F32 = jnp.float32
NLON = 1440
NZ = 8
LON = 180
MODES = 720
MP = 384
KP = 768
CB = 16
NK = 3
NR = 4
WIDE = 896
LIMIT = 24 * 1024 * 1024


def dft_table():
    lane = np.arange(KP)
    tail = lane >= 512
    owner = np.where(tail, 2 * ((lane - 512) // 128) + (lane % 128 >= 64), lane // 128)
    place = np.where(tail, 128 + lane % 64, lane % 128)
    column = owner * LON + place
    tables = []
    for parity in range(2):
        frequency = 2 * np.arange(MP) + parity
        phase = 2.0 * math.pi * ((column[:, None] * frequency[None, :]) % NLON) / NLON
        valid = (place < LON)[:, None] & (frequency < MODES)[None, :]
        cos = np.where(valid, np.cos(phase), 0.0)
        sin = np.where(valid, -np.sin(phase), 0.0)
        tables.append(np.concatenate([cos, sin], axis=1))
    return np.stack(tables).astype(ml_dtypes.bfloat16)


def dot(a, b):
    return jnp.dot(a, b, preferred_element_type=F32)


def dot_tn(a, b):
    return lax.dot_general(a, b, (((0,), (0,)), ((), ())), preferred_element_type=F32)


def dot_nt(a, b):
    return lax.dot_general(a, b, (((1,), (1,)), ((), ())), preferred_element_type=F32)


def low_halves(a, b):
    return jnp.concatenate([a[:, :64], b[:, :64]], axis=1)


def high_halves(a, b):
    return jnp.concatenate([a[:, 64:], b[:, 64:]], axis=1)


def iota(shape, dim):
    return lax.broadcasted_iota(jnp.int32, shape, dim)


def point_select():
    lane = iota((8, 2 * 384), 1)
    first = (lane >= 384).astype(jnp.int32)
    lane = lane - 384 * first
    middle = (lane >= 128) & (lane < 256)
    upper = ((lane >= 192)).astype(jnp.int32)
    place = jnp.where(middle, 128 + (lane & 63), lane & 127)
    point = jnp.where(place < LON, place * NR + 2 * upper + first, -1)
    return (iota((LON * NR, 2 * 384), 0) == point[0:1]).astype(F32).astype(BF)


def tile_of(z):
    return 6 * (z // 4) + z % 4


def tile_of_pair(pair):
    return 6 * (pair // 2) + 4 + pair % 2


def unpack(ref, x_ref, base, rows):
    for z in range(NZ):
        lanes = slice(128 * tile_of(z), 128 * tile_of(z) + 128)
        x_ref[base : base + rows, lanes] = ref[z, :, 0:128]
        x_ref[base + rows : base + 2 * rows, lanes] = ref[z, :, 256:384]
    for pair in range(NZ // 2):
        lanes = slice(128 * tile_of_pair(pair), 128 * tile_of_pair(pair) + 128)
        even = ref[2 * pair, :, 128:256]
        odd = ref[2 * pair + 1, :, 128:256]
        x_ref[base : base + rows, lanes] = low_halves(even, odd)
        x_ref[base + rows : base + 2 * rows, lanes] = high_halves(even, odd)


def pack(ref, half, value, rows):
    for t in range(4):
        lanes = slice(128 * t, 128 * t + 128)
        ref[4 * half + t, :, 0:128] = value[:rows, lanes]
        ref[4 * half + t, :, 256:384] = value[rows:, lanes]
    for t in range(2):
        lanes = slice(512 + 128 * t, 640 + 128 * t)
        lower, upper = value[:rows, lanes], value[rows:, lanes]
        ref[4 * half + 2 * t, :, 128:256] = low_halves(lower, upper)
        ref[4 * half + 2 * t + 1, :, 128:256] = high_halves(lower, upper)


def bring(pairs, sems):
    copies = [
        pltpu.make_async_copy(source, target, sems.at[n]) for n, (source, target) in enumerate(pairs)
    ]
    for copy in copies:
        copy.start()
    return copies


def pack_kernel(points_hbm, wide_ref, send_ref, points_ref, sems):
    copies = bring([(points_hbm, points_ref)], sems)
    select = point_select()
    copies[0].wait()
    wide = dot_tn(points_ref[...], select).astype(BF)
    wide_ref[...] = wide
    for s in range(NZ):
        for first in range(2):
            send_ref[s, CB * first : CB * first + CB, :] = wide[
                CB * s : CB * s + CB, 384 * first : 384 * first + 384
            ]


def prepare_kernel(
    points_hbm,
    weights_hbm,
    real_hbm,
    imag_hbm,
    support_hbm,
    wide_ref,
    coupling_ref,
    turned_hbm,
    gain_ref,
    turned_ref,
    points_ref,
    weights_ref,
    real_ref,
    imag_ref,
    support_ref,
    sems,
):
    copies = bring(
        (
            (points_hbm, points_ref),
            (weights_hbm, weights_ref),
            (real_hbm, real_ref),
            (imag_hbm, imag_ref),
            (support_hbm, support_ref),
        ),
        sems,
    )
    select = point_select()
    copies[0].wait()
    wide_ref[...] = dot_tn(points_ref[...], select).astype(BF)

    for copy in copies[1:]:
        copy.wait()
    flip = lax.rem(lax.axis_index("lat"), 2) == 0
    lane = iota((1, 12), 1)
    seen = support_ref[...]
    seen = jnp.where(lane < 4, seen[:, 0:1], jnp.where(lane < 8, seen[:, 1:2], seen[:, 2:3]))
    seen = seen.astype(F32)
    rows = [weights_ref[k].astype(F32) for k in range(NK)]
    masked = jnp.concatenate([rows[k][i : i + 1] * seen for i in range(NR) for k in range(NK)], axis=0)
    turned = jnp.concatenate([masked[:, 8:12], masked[:, 4:8], masked[:, 0:4]], axis=1)
    masked = jnp.where(flip, turned, masked).astype(BF)
    size = 12 * CB
    expand = (iota((size, 12), 0) // CB == iota((size, 12), 1)).astype(F32).astype(BF)
    same = (iota((size, size), 0) & 15) == (iota((size, size), 1) & 15)
    wide = dot_nt(dot(expand, masked).astype(BF), expand)
    coupling_ref[...] = jnp.where(same, wide, 0.0).astype(BF)
    wide = dot_nt(dot_nt(expand, masked).astype(BF), expand)
    turned_ref[...] = jnp.where(same, wide, 0.0).astype(BF)
    copies = bring([(turned_ref, turned_hbm)], sems)

    lane = iota((MODES, 2 * MP), 1)
    odd = (lane >= MP).astype(jnp.int32)
    split = (iota((MODES, 2 * MP), 0) == 2 * (lane - MP * odd) + odd).astype(F32).astype(BF)
    first_half = jnp.where(iota((1, 2 * MP), 1) == 0, 0.5, 1.0).astype(F32)
    rest = []
    for ref in (real_ref, imag_ref):
        rows = [ref[k] for k in range(NK)]
        rest += [rows[k][i : i + 1] for i in range(NR) for k in range(NK)]
    rest = jnp.concatenate(rest, axis=0)
    pieces = []
    for step in range(3):
        piece = rest.astype(BF)
        rest = rest - piece.astype(F32)
        pieces.append(piece.astype(F32))
    moved = dot(jnp.concatenate(pieces, axis=0).astype(BF), split)
    gain_ref[...] = (moved[0:24] + moved[24:48] + moved[48:72]) * first_half
    copies[0].wait()


def spectral(value, parity, table_ref, gain_ref, filt_ref, sign):
    spec = dot(value, table_ref[parity])
    lanes = slice(MP * parity, MP * parity + MP)
    for g in range(12):
        rows = slice(CB * g, CB * g + CB)
        part_a, part_b = spec[rows, :MP], spec[rows, MP:]
        real = gain_ref[g : g + 1, lanes]
        imag = sign * gain_ref[12 + g : 13 + g, lanes]
        filt_ref[parity, rows, :MP] = (real * part_a - imag * part_b).astype(BF)
        filt_ref[parity, rows, MP:] = (real * part_b + imag * part_a).astype(BF)


def transform(lower, upper, table_ref, gain_ref, filt_ref, sign, copies):
    for parity, value in enumerate((lower + upper, lower - upper)):
        copies[parity].wait()
        spectral(value.astype(BF), parity, table_ref, gain_ref, filt_ref, sign)
    even = dot_nt(filt_ref[0], table_ref[0])
    odd = dot_nt(filt_ref[1], table_ref[1])
    scale = 2.0 / NLON
    return ((even + odd) * scale).astype(BF), ((even - odd) * scale).astype(BF)


def filter_kernel(
    first_ref,
    own_ref,
    second_ref,
    coupling_ref,
    gain_ref,
    table_hbm,
    send_ref,
    x_ref,
    filt_ref,
    table_ref,
    sems,
):
    copies = bring([(table_hbm.at[p], table_ref.at[p]) for p in range(2)], sems)
    for band, ref in enumerate((first_ref, own_ref, second_ref)):
        unpack(ref, x_ref, 64 * band, 32)
    coupling = coupling_ref[...]
    lower = dot(coupling, x_ref[:, :KP])
    upper = dot(coupling, x_ref[:, KP:])
    lower, upper = transform(lower, upper, table_ref, gain_ref, filt_ref, 1.0, copies)
    pack(send_ref, 0, lower, 96)
    pack(send_ref, 1, upper, 96)


def gelu_parts(hidden):
    inner_part = GELU_SCALE * (hidden + CUBIC_TERM * hidden * hidden * hidden)
    tangent = jnp.tanh(inner_part)
    gelu_value = 0.5 * hidden * (1.0 + tangent)
    gelu_slope = 0.5 * (1.0 + tangent) + 0.5 * hidden * (1.0 - tangent * tangent) * GELU_SCALE * (
        1.0 + 3.0 * CUBIC_TERM * hidden * hidden
    )
    return (gelu_value, gelu_slope)


def mlp_kernel(
    recv_ref,
    fields_ref,
    cot_ref,
    filter_ref,
    inner_ref,
    outer_ref,
    back_hbm,
    grads_hbm,
    state_grad_hbm,
    back_ref,
    grads_ref,
    state_grad_ref,
    sems,
):
    mix = jnp.concatenate(
        [filter_ref[k, CB * s : CB * s + CB, :] for s in range(NZ) for k in range(NK)], axis=0
    )
    inner = inner_ref[...]
    outer = outer_ref[...]
    held = []
    for first in range(2):
        lanes = slice(384 * first, 384 * first + 384)
        filtered = jnp.concatenate(
            [recv_ref[s, 48 * first : 48 * first + 48, :] for s in range(NZ)], axis=0
        )
        cot = cot_ref[:, lanes]
        state = (fields_ref[:, lanes].astype(F32) + dot_tn(mix, filtered)).astype(BF)
        hidden = dot_tn(inner, state)
        value, slope = gelu_parts(hidden)
        active = value.astype(BF)
        d_hidden = (dot(outer, cot) * slope).astype(BF)
        d_state = cot.astype(F32) + dot(inner, d_hidden)
        state_grad_ref[:, lanes] = d_state
        d_state_b = d_state.astype(BF)
        for tile in range(3):
            base = 256 * tile + 128 * first
            back_ref[base : base + 128, :] = d_state_b[:, 128 * tile : 128 * tile + 128]
        held.append((filtered, d_state_b, active, cot, state, d_hidden))
    copies = bring(((back_ref, back_hbm), (state_grad_ref, state_grad_hbm)), sems)
    sums = None
    for filtered, d_state_b, active, cot, state, d_hidden in held:
        parts = (dot_nt(filtered, d_state_b), dot_nt(active, cot), dot_nt(state, d_hidden))
        sums = parts if sums is None else tuple(a + b for a, b in zip(sums, parts))
    grads_ref[0:384, :] = sums[0].astype(BF)
    grads_ref[384:640, :] = sums[1].astype(BF)
    grads_ref[640:768, :] = sums[2][:, :128].astype(BF)
    grads_ref[768:896, :] = sums[2][:, 128:].astype(BF)
    last = pltpu.make_async_copy(grads_ref, grads_hbm, sems.at[2])
    last.start()
    for copy in copies + [last]:
        copy.wait()


def adjoint_kernel(
    recv_hbm,
    turned_hbm,
    state_grad_hbm,
    gain_ref,
    table_ref,
    filter_ref,
    first_ref,
    base_hbm,
    second_ref,
    x_ref,
    middle_ref,
    spec_ref,
    filt_ref,
    held_ref,
    part_ref,
    turned_ref,
    state_grad_ref,
    base_ref,
    sems,
):
    pairs = [(recv_hbm.at[n, pl.ds(256, 256), :], middle_ref.at[n]) for n in range(NZ)]
    for half in range(2):
        for n in range(NZ):
            lanes = pl.ds(128 * tile_of(n), 128)
            rows = pl.ds(256 * half, 256)
            pairs.append((recv_hbm.at[n, pl.ds(512 * half, 256), :], x_ref.at[rows, lanes]))
    pairs += [(turned_hbm, turned_ref), (state_grad_hbm, state_grad_ref)]
    copies = bring(pairs, sems)
    z = lax.axis_index("lon")
    quarter = lax.rem(z, 4)
    sign = jnp.where(z < 4, 1.0, -1.0)
    main = pl.ds(pl.multiple_of(128 * quarter, 128), 128)
    tail = pl.ds(pl.multiple_of(512 + 64 * quarter, 64), 64)
    places = [
        jnp.concatenate([table_ref[p, main, :], table_ref[p, tail, :]], axis=0) for p in range(2)
    ]
    for half in range(2):
        for copy in copies[0 : 2 * NZ] if half == 0 else copies[2 * NZ :]:
            copy.wait()
        block = slice(256 * half, 256 * half + 256)
        for pair in range(NZ // 2):
            lanes = slice(128 * tile_of_pair(pair), 128 * tile_of_pair(pair) + 128)
            even, odd = middle_ref[2 * pair], middle_ref[2 * pair + 1]
            x_ref[block, lanes] = low_halves(even, odd) if half == 0 else high_halves(even, odd)
        lower = x_ref[block, :KP].astype(F32)
        upper = x_ref[block, KP:].astype(F32)
        spec_ref[0, block, :] = dot((lower + upper).astype(BF), table_ref[0])
        spec_ref[1, block, :] = dot((lower - upper).astype(BF), table_ref[1])
        for i in (2 * half, 2 * half + 1):
            rows = slice(128 * i, 128 * i + 128)
            for parity in range(2):
                lanes = slice(MP * parity, MP * parity + MP)
                part_a, part_b = spec_ref[parity, rows, :MP], spec_ref[parity, rows, MP:]
                for k in range(NK):
                    g = NK * i + k
                    real = gain_ref[g : g + 1, lanes]
                    imag = gain_ref[12 + g : 13 + g, lanes]
                    out = slice(128 * k, 128 * k + 128)
                    filt_ref[i, parity, out, :MP] = (real * part_a + imag * part_b).astype(BF)
                    filt_ref[i, parity, out, MP:] = (real * part_b - imag * part_a).astype(BF)
            result = dot_nt(filt_ref[i, 0], places[0]) + sign * dot_nt(filt_ref[i, 1], places[1])
            result = (result * (2.0 / NLON)).astype(BF)
            held_ref[:, 192 * i : 192 * i + 192] = result
    for k in range(NK):
        mixed = dot(filter_ref[k], held_ref[128 * k : 128 * k + 128, :]).astype(BF)
        for i in range(NR):
            part_ref[NK * i + k] = mixed[:, 192 * i : 192 * i + 192]
    copies = []
    for s in range(NZ):
        rows = slice(CB * s, CB * s + CB)
        parts = jnp.concatenate([part_ref[g, rows, :] for g in range(12)], axis=0)
        total = dot(turned_ref[...], parts)
        for band, ref in enumerate((first_ref, base_ref, second_ref)):
            for first in range(2):
                base = 64 * band + CB * first
                lower, upper = total[base : base + CB], total[base + 32 : base + 32 + CB]
                middle = jnp.concatenate([lower[:, 128:], upper[:, 128:]], axis=1)
                for tile, value in enumerate((lower[:, :128], middle, upper[:, :128])):
                    lanes = slice(384 * first + 128 * tile, 384 * first + 128 * tile + 128)
                    if band == 1:
                        ref[rows, lanes] = value + state_grad_ref[rows, lanes]
                    else:
                        ref[rows, lanes] = value.astype(BF)
        piece = pl.ds(CB * s, CB)
        copies.append(
            pltpu.make_async_copy(base_ref.at[piece], base_hbm.at[piece], sems.at[s])
        )
        copies[-1].start()
    for copy in copies:
        copy.wait()


def sum_kernel(share, recv_ref, out_ref):
    rows, columns = out_ref.shape[0], recv_ref.shape[0]
    same = lax.rem(iota((rows, columns), 0), share) == lax.rem(iota((rows, columns), 1), share)
    out_ref[...] = dot(same.astype(F32).astype(BF), recv_ref[...]).astype(BF)


def field_kernel(base_hbm, first_ref, second_ref, grad_ref, base_ref, sems):
    copies = bring([(base_hbm, base_ref)], sems)
    select = point_select()
    halo = first_ref[...].astype(F32) + second_ref[...].astype(F32)
    copies[0].wait()
    grad_ref[...] = dot_nt(select, (base_ref[...] + halo).astype(BF)).astype(BF)


def weights_kernel(scale, grads_ref, filter_ref, inner_ref, outer_ref):
    for s in range(NZ):
        for k in range(NK):
            base = 48 * s + CB * k
            filter_ref[k, CB * s : CB * s + CB, :] = grads_ref[base : base + CB, :].astype(F32) * scale
    outer_ref[...] = grads_ref[384:640, :].astype(F32) * scale
    inner_ref[:, :128] = grads_ref[640:768, :].astype(F32) * scale
    inner_ref[:, 128:] = grads_ref[768:896, :].astype(F32) * scale


def call(kernel, outs, flops, scratch=(), in_specs=None, out_specs=None):
    shapes = outs if isinstance(outs, tuple) else (outs,)
    moved = sum(math.prod(o.shape) * o.dtype.itemsize for o in shapes)
    if out_specs is None:
        out_specs = jax.tree.map(lambda _: pl.BlockSpec(memory_space=pltpu.VMEM), outs)
    return pl.pallas_call(
        kernel,
        out_shape=outs,
        in_specs=in_specs,
        out_specs=out_specs,
        scratch_shapes=scratch,
        compiler_params=pltpu.CompilerParams(vmem_limit_bytes=LIMIT),
        cost_estimate=pl.CostEstimate(flops=flops, bytes_accessed=2 * moved, transcendentals=0),
    )


def shaped(shape, dtype=BF):
    return jax.ShapeDtypeStruct(shape, dtype)


def in_hbm(shape, dtype=BF):
    return pltpu.HBM(shape, dtype)


def hold(value):
    return pltpu.with_memory_space_constraint(value, pltpu.HBM)


def vmem(count):
    return [pl.BlockSpec(memory_space=pltpu.VMEM)] * count


def hbm(count):
    return [pl.BlockSpec(memory_space=pltpu.HBM)] * count


def swapped(value, first):
    count = lax.axis_size("lat")
    pairs = []
    for low in range(first, count - 1, 2):
        pairs += [(low, low + 1), (low + 1, low)]
    return lax.ppermute(value, "lat", pairs)


def local(
    fields,
    cotangent,
    basis_weights,
    band_support,
    spectrum_real,
    spectrum_imag,
    filter_weights,
    inner_weights,
    outer_weights,
):
    group = lax.axis_size("ens") * lax.axis_size("lat")
    grad_scale = 1.0 / math.sqrt(group * NR * NLON)
    table = jnp.asarray(dft_table())

    field_points = fields[0].transpose(1, 0, 2).reshape(LON * NR, 128)
    cot_points = cotangent[0].transpose(1, 0, 2).reshape(LON * NR, 128)
    field_wide, send_fields = call(
        pack_kernel, (shaped((128, 768)), shaped((NZ, 32, 384))), 2 * 720 * 768 * 128,
        [pltpu.VMEM((720, 128), BF), pltpu.SemaphoreType.DMA((1,))], hbm(1)
    )(hold(field_points))
    own = lax.all_to_all(send_fields, "lon", 0, 0, tiled=True)

    cot_wide, coupling, turned, gains = call(
        prepare_kernel,
        (
            shaped((128, 768)),
            shaped((192, 192)),
            in_hbm((192, 192)),
            shaped((24, 2 * MP), F32),
        ),
        2 * 720 * 768 * 128,
        [
            pltpu.VMEM((192, 192), BF),
            pltpu.VMEM((720, 128), BF),
            pltpu.VMEM((NK, NR, 12), BF),
            pltpu.VMEM((NK, NR, MODES), F32),
            pltpu.VMEM((NK, NR, MODES), F32),
            pltpu.VMEM((1, 3), jnp.int32),
            pltpu.SemaphoreType.DMA((5,)),
        ],
        hbm(5),
        tuple(vmem(2) + hbm(1) + vmem(1)),
    )(
        hold(cot_points),
        hold(basis_weights),
        hold(spectrum_real),
        hold(spectrum_imag),
        hold(band_support),
    )

    first = swapped(own, 0)
    second = swapped(own, 1)
    work = [
        pltpu.VMEM((192, 2 * KP), BF),
        pltpu.VMEM((2, 192, 2 * MP), BF),
        pltpu.VMEM((2, KP, 2 * MP), BF),
        pltpu.SemaphoreType.DMA((3,)),
    ]
    send_filtered = call(
        filter_kernel, shaped((NZ, 96, 384)), 8 * 192 * KP * KP, work, vmem(5) + hbm(1)
    )(first, own, second, coupling, gains, hold(table))
    filtered = lax.all_to_all(send_filtered, "lon", 0, 0, tiled=True)

    back, grads, state_grad = call(
        mlp_kernel,
        (in_hbm((768, 128)), in_hbm((WIDE, 128)), in_hbm((128, 768), F32)),
        2 * 768 * 128 * 256 * 10,
        [
            pltpu.VMEM((768, 128), BF),
            pltpu.VMEM((WIDE, 128), BF),
            pltpu.VMEM((128, 768), F32),
            pltpu.SemaphoreType.DMA((3,)),
        ],
        vmem(6),
        tuple(hbm(3)),
    )(filtered, field_wide, cot_wide, filter_weights, inner_weights, outer_weights)
    back = lax.all_gather(back, "lon", tiled=True).reshape(NZ, 768, 128)

    share = WIDE // group

    def exchanged(value, axes):
        value = value.reshape(value.shape[0] // 2, 2, 128)
        return lax.all_to_all(value, axes, 0, 0, tiled=True).reshape(-1, 128)

    def summed(value, copies):
        return call(
            functools.partial(sum_kernel, share),
            shaped((copies * share, 128)),
            2 * copies * share * value.size,
            (),
            vmem(1),
        )(value)

    chunks = exchanged(grads, ("ens", "lat"))
    chunks = exchanged(summed(chunks, NZ), "lon")
    gathered = exchanged(summed(chunks, group), ("ens", "lat"))

    to_first, kept, to_second = call(
        adjoint_kernel,
        (shaped((128, 768)), in_hbm((128, 768), F32), shaped((128, 768))),
        4 * 512 * KP * KP + 4 * 1536 * KP * 192,
        [
            pltpu.VMEM((512, 2 * KP), BF),
            pltpu.VMEM((NZ, 256, 128), BF),
            pltpu.VMEM((2, 512, 2 * MP), F32),
            pltpu.VMEM((NR, 2, 384, 2 * MP), BF),
            pltpu.VMEM((384, 768), BF),
            pltpu.VMEM((12, 128, 192), BF),
            pltpu.VMEM((192, 192), BF),
            pltpu.VMEM((128, 768), F32),
            pltpu.VMEM((128, 768), F32),
            pltpu.SemaphoreType.DMA((3 * NZ + 2,)),
        ],
        hbm(3) + vmem(3),
        tuple(vmem(1) + hbm(1) + vmem(1)),
    )(hold(back), hold(turned), hold(state_grad), gains, table, filter_weights)
    from_second = swapped(to_second, 1)
    from_first = swapped(to_first, 0)
    grad_points = call(
        field_kernel,
        shaped((LON * NR, 128)),
        2 * 720 * 768 * 128,
        [pltpu.VMEM((128, 768), F32), pltpu.SemaphoreType.DMA((1,))],
        hbm(1) + vmem(2),
    )(hold(kept), from_second, from_first)

    filter_grad, inner_grad, outer_grad = call(
        functools.partial(weights_kernel, grad_scale),
        (shaped((NK, 128, 128), F32), shaped((128, 256), F32), shaped((256, 128), F32)),
        WIDE * 128,
        (),
        vmem(1),
    )(gathered)
    field_grad = grad_points.reshape(LON, NR, 128).transpose(1, 0, 2)[None]
    return (field_grad, filter_grad, inner_grad, outer_grad)


def solution(mesh):
    placed = (
        P("ens", "lat", "lon", None),
        P("ens", "lat", "lon", None),
        P(None, "lat", None),
        P("lat", None),
        P(None, "lat", None),
        P(None, "lat", None),
        P(),
        P(),
        P(),
    )
    return jax.shard_map(
        local,
        mesh=mesh,
        in_specs=placed,
        out_specs=(P("ens", "lat", "lon", None), P(), P(), P()),
        check_vma=False,
    )
```

```python
import functools
import math

import jax
import jax.numpy as jnp
import ml_dtypes
import numpy as np
from jax import lax
from jax.experimental import pallas as pl
from jax.experimental.pallas import tpu as pltpu
from jax.sharding import PartitionSpec as P

GELU_SCALE = 0.7978845608028654
CUBIC_TERM = 0.044715
BF = jnp.bfloat16
F32 = jnp.float32
NLON = 1440
NZ = 8
LON = 180
MODES = 720
MP = 384
KP = 768
CB = 16
NK = 3
NR = 4
WIDE = 896
LIMIT = 24 * 1024 * 1024


def dft_table():
    lane = np.arange(KP)
    tail = lane >= 512
    owner = np.where(tail, 2 * ((lane - 512) // 128) + (lane % 128 >= 64), lane // 128)
    place = np.where(tail, 128 + lane % 64, lane % 128)
    column = owner * LON + place
    tables = []
    for parity in range(2):
        frequency = 2 * np.arange(MP) + parity
        phase = 2.0 * math.pi * ((column[:, None] * frequency[None, :]) % NLON) / NLON
        valid = (place < LON)[:, None] & (frequency < MODES)[None, :]
        cos = np.where(valid, np.cos(phase), 0.0)
        sin = np.where(valid, -np.sin(phase), 0.0)
        tables.append(np.concatenate([cos, sin], axis=1))
    return np.stack(tables).astype(ml_dtypes.bfloat16)


def dot(a, b):
    return jnp.dot(a, b, preferred_element_type=F32)


def dot_tn(a, b):
    return lax.dot_general(a, b, (((0,), (0,)), ((), ())), preferred_element_type=F32)


def dot_nt(a, b):
    return lax.dot_general(a, b, (((1,), (1,)), ((), ())), preferred_element_type=F32)


def low_halves(a, b):
    return jnp.concatenate([a[:, :64], b[:, :64]], axis=1)


def high_halves(a, b):
    return jnp.concatenate([a[:, 64:], b[:, 64:]], axis=1)


def iota(shape, dim):
    return lax.broadcasted_iota(jnp.int32, shape, dim)


def point_select():
    lane = iota((8, 2 * 384), 1)
    first = (lane >= 384).astype(jnp.int32)
    lane = lane - 384 * first
    middle = (lane >= 128) & (lane < 256)
    upper = ((lane >= 192)).astype(jnp.int32)
    place = jnp.where(middle, 128 + (lane & 63), lane & 127)
    point = jnp.where(place < LON, place * NR + 2 * upper + first, -1)
    return (iota((LON * NR, 2 * 384), 0) == point[0:1]).astype(F32).astype(BF)


def tile_of(z):
    return 6 * (z // 4) + z % 4


def tile_of_pair(pair):
    return 6 * (pair // 2) + 4 + pair % 2


def unpack(ref, x_ref, base, rows):
    for z in range(NZ):
        lanes = slice(128 * tile_of(z), 128 * tile_of(z) + 128)
        x_ref[base : base + rows, lanes] = ref[z, :, 0:128]
        x_ref[base + rows : base + 2 * rows, lanes] = ref[z, :, 256:384]
    for pair in range(NZ // 2):
        lanes = slice(128 * tile_of_pair(pair), 128 * tile_of_pair(pair) + 128)
        even = ref[2 * pair, :, 128:256]
        odd = ref[2 * pair + 1, :, 128:256]
        x_ref[base : base + rows, lanes] = low_halves(even, odd)
        x_ref[base + rows : base + 2 * rows, lanes] = high_halves(even, odd)


def pack(ref, half, value, rows):
    for t in range(4):
        lanes = slice(128 * t, 128 * t + 128)
        ref[4 * half + t, :, 0:128] = value[:rows, lanes]
        ref[4 * half + t, :, 256:384] = value[rows:, lanes]
    for t in range(2):
        lanes = slice(512 + 128 * t, 640 + 128 * t)
        lower, upper = value[:rows, lanes], value[rows:, lanes]
        ref[4 * half + 2 * t, :, 128:256] = low_halves(lower, upper)
        ref[4 * half + 2 * t + 1, :, 128:256] = high_halves(lower, upper)


def bring(pairs, sems):
    copies = [
        pltpu.make_async_copy(source, target, sems.at[n]) for n, (source, target) in enumerate(pairs)
    ]
    for copy in copies:
        copy.start()
    return copies


def pack_kernel(points_hbm, wide_ref, send_ref, points_ref, sems):
    copies = bring([(points_hbm, points_ref)], sems)
    select = point_select()
    copies[0].wait()
    wide = dot_tn(points_ref[...], select).astype(BF)
    wide_ref[...] = wide
    for s in range(NZ):
        for first in range(2):
            send_ref[s, CB * first : CB * first + CB, :] = wide[
                CB * s : CB * s + CB, 384 * first : 384 * first + 384
            ]


def prepare_kernel(
    points_hbm,
    weights_hbm,
    real_hbm,
    imag_hbm,
    support_hbm,
    wide_ref,
    coupling_ref,
    turned_hbm,
    gain_ref,
    turned_ref,
    points_ref,
    weights_ref,
    real_ref,
    imag_ref,
    support_ref,
    sems,
):
    copies = bring(
        (
            (points_hbm, points_ref),
            (weights_hbm, weights_ref),
            (real_hbm, real_ref),
            (imag_hbm, imag_ref),
            (support_hbm, support_ref),
        ),
        sems,
    )
    select = point_select()
    copies[0].wait()
    wide_ref[...] = dot_tn(points_ref[...], select).astype(BF)

    for copy in copies[1:]:
        copy.wait()
    flip = lax.rem(lax.axis_index("lat"), 2) == 0
    lane = iota((1, 12), 1)
    seen = support_ref[...]
    seen = jnp.where(lane < 4, seen[:, 0:1], jnp.where(lane < 8, seen[:, 1:2], seen[:, 2:3]))
    seen = seen.astype(F32)
    rows = [weights_ref[k].astype(F32) for k in range(NK)]
    masked = jnp.concatenate([rows[k][i : i + 1] * seen for i in range(NR) for k in range(NK)], axis=0)
    turned = jnp.concatenate([masked[:, 8:12], masked[:, 4:8], masked[:, 0:4]], axis=1)
    masked = jnp.where(flip, turned, masked).astype(BF)
    size = 12 * CB
    expand = (iota((size, 12), 0) // CB == iota((size, 12), 1)).astype(F32).astype(BF)
    same = (iota((size, size), 0) & 15) == (iota((size, size), 1) & 15)
    wide = dot_nt(dot(expand, masked).astype(BF), expand)
    coupling_ref[...] = jnp.where(same, wide, 0.0).astype(BF)
    wide = dot_nt(dot_nt(expand, masked).astype(BF), expand)
    turned_ref[...] = jnp.where(same, wide, 0.0).astype(BF)
    copies = bring([(turned_ref, turned_hbm)], sems)

    lane = iota((MODES, 2 * MP), 1)
    odd = (lane >= MP).astype(jnp.int32)
    split = (iota((MODES, 2 * MP), 0) == 2 * (lane - MP * odd) + odd).astype(F32).astype(BF)
    first_half = jnp.where(iota((1, 2 * MP), 1) == 0, 0.5, 1.0).astype(F32)
    rest = []
    for ref in (real_ref, imag_ref):
        rows = [ref[k] for k in range(NK)]
        rest += [rows[k][i : i + 1] for i in range(NR) for k in range(NK)]
    rest = jnp.concatenate(rest, axis=0)
    pieces = []
    for step in range(3):
        piece = rest.astype(BF)
        rest = rest - piece.astype(F32)
        pieces.append(piece.astype(F32))
    moved = dot(jnp.concatenate(pieces, axis=0).astype(BF), split)
    gain_ref[...] = (moved[0:24] + moved[24:48] + moved[48:72]) * first_half
    copies[0].wait()


def spectral(value, parity, table_ref, gain_ref, filt_ref, sign):
    spec = dot(value, table_ref[parity])
    lanes = slice(MP * parity, MP * parity + MP)
    for g in range(12):
        rows = slice(CB * g, CB * g + CB)
        part_a, part_b = spec[rows, :MP], spec[rows, MP:]
        real = gain_ref[g : g + 1, lanes]
        imag = sign * gain_ref[12 + g : 13 + g, lanes]
        filt_ref[parity, rows, :MP] = (real * part_a - imag * part_b).astype(BF)
        filt_ref[parity, rows, MP:] = (real * part_b + imag * part_a).astype(BF)


def transform(lower, upper, table_ref, gain_ref, filt_ref, sign, copies):
    for parity, value in enumerate((lower + upper, lower - upper)):
        copies[parity].wait()
        spectral(value.astype(BF), parity, table_ref, gain_ref, filt_ref, sign)
    even = dot_nt(filt_ref[0], table_ref[0])
    odd = dot_nt(filt_ref[1], table_ref[1])
    scale = 2.0 / NLON
    return ((even + odd) * scale).astype(BF), ((even - odd) * scale).astype(BF)


def filter_kernel(
    first_ref,
    own_ref,
    second_ref,
    coupling_ref,
    gain_ref,
    table_hbm,
    send_ref,
    x_ref,
    filt_ref,
    table_ref,
    sems,
):
    copies = bring([(table_hbm.at[p], table_ref.at[p]) for p in range(2)], sems)
    for band, ref in enumerate((first_ref, own_ref, second_ref)):
        unpack(ref, x_ref, 64 * band, 32)
    coupling = coupling_ref[...]
    lower = dot(coupling, x_ref[:, :KP])
    upper = dot(coupling, x_ref[:, KP:])
    lower, upper = transform(lower, upper, table_ref, gain_ref, filt_ref, 1.0, copies)
    pack(send_ref, 0, lower, 96)
    pack(send_ref, 1, upper, 96)


def gelu_parts(hidden):
    inner_part = GELU_SCALE * (hidden + CUBIC_TERM * hidden * hidden * hidden)
    tangent = jnp.tanh(inner_part)
    gelu_value = 0.5 * hidden * (1.0 + tangent)
    gelu_slope = 0.5 * (1.0 + tangent) + 0.5 * hidden * (1.0 - tangent * tangent) * GELU_SCALE * (
        1.0 + 3.0 * CUBIC_TERM * hidden * hidden
    )
    return (gelu_value, gelu_slope)


def mlp_kernel(
    recv_ref,
    fields_ref,
    cot_ref,
    filter_ref,
    inner_ref,
    outer_ref,
    back_hbm,
    grads_hbm,
    state_grad_hbm,
    back_ref,
    grads_ref,
    state_grad_ref,
    sems,
):
    mix = jnp.concatenate(
        [filter_ref[k, CB * s : CB * s + CB, :] for s in range(NZ) for k in range(NK)], axis=0
    )
    inner = inner_ref[...]
    outer = outer_ref[...]
    held = []
    for first in range(2):
        lanes = slice(384 * first, 384 * first + 384)
        filtered = jnp.concatenate(
            [recv_ref[s, 48 * first : 48 * first + 48, :] for s in range(NZ)], axis=0
        )
        cot = cot_ref[:, lanes]
        state = (fields_ref[:, lanes].astype(F32) + dot_tn(mix, filtered)).astype(BF)
        hidden = dot_tn(inner, state)
        value, slope = gelu_parts(hidden)
        active = value.astype(BF)
        d_hidden = (dot(outer, cot) * slope).astype(BF)
        d_state = cot.astype(F32) + dot(inner, d_hidden)
        state_grad_ref[:, lanes] = d_state
        d_state_b = d_state.astype(BF)
        for tile in range(3):
            base = 256 * tile + 128 * first
            back_ref[base : base + 128, :] = d_state_b[:, 128 * tile : 128 * tile + 128]
        held.append((filtered, d_state_b, active, cot, state, d_hidden))
    copies = bring(((back_ref, back_hbm), (state_grad_ref, state_grad_hbm)), sems)
    sums = None
    for filtered, d_state_b, active, cot, state, d_hidden in held:
        parts = (dot_nt(filtered, d_state_b), dot_nt(active, cot), dot_nt(state, d_hidden))
        sums = parts if sums is None else tuple(a + b for a, b in zip(sums, parts))
    grads_ref[0:384, :] = sums[0].astype(BF)
    grads_ref[384:640, :] = sums[1].astype(BF)
    grads_ref[640:768, :] = sums[2][:, :128].astype(BF)
    grads_ref[768:896, :] = sums[2][:, 128:].astype(BF)
    last = pltpu.make_async_copy(grads_ref, grads_hbm, sems.at[2])
    last.start()
    for copy in copies + [last]:
        copy.wait()


def adjoint_kernel(
    recv_hbm,
    turned_hbm,
    state_grad_hbm,
    gain_ref,
    table_ref,
    filter_ref,
    first_ref,
    base_hbm,
    second_ref,
    x_ref,
    middle_ref,
    spec_ref,
    filt_ref,
    held_ref,
    part_ref,
    turned_ref,
    state_grad_ref,
    base_ref,
    sems,
):
    pairs = [(recv_hbm.at[n, pl.ds(256, 256), :], middle_ref.at[n]) for n in range(NZ)]
    for half in range(2):
        for n in range(NZ):
            lanes = pl.ds(128 * tile_of(n), 128)
            rows = pl.ds(256 * half, 256)
            pairs.append((recv_hbm.at[n, pl.ds(512 * half, 256), :], x_ref.at[rows, lanes]))
    pairs += [(turned_hbm, turned_ref), (state_grad_hbm, state_grad_ref)]
    copies = bring(pairs, sems)
    z = lax.axis_index("lon")
    quarter = lax.rem(z, 4)
    sign = jnp.where(z < 4, 1.0, -1.0)
    main = pl.ds(pl.multiple_of(128 * quarter, 128), 128)
    tail = pl.ds(pl.multiple_of(512 + 64 * quarter, 64), 64)
    places = [
        jnp.concatenate([table_ref[p, main, :], table_ref[p, tail, :]], axis=0) for p in range(2)
    ]
    for half in range(2):
        for copy in copies[0 : 2 * NZ] if half == 0 else copies[2 * NZ :]:
            copy.wait()
        block = slice(256 * half, 256 * half + 256)
        for pair in range(NZ // 2):
            lanes = slice(128 * tile_of_pair(pair), 128 * tile_of_pair(pair) + 128)
            even, odd = middle_ref[2 * pair], middle_ref[2 * pair + 1]
            x_ref[block, lanes] = low_halves(even, odd) if half == 0 else high_halves(even, odd)
        lower = x_ref[block, :KP].astype(F32)
        upper = x_ref[block, KP:].astype(F32)
        spec_ref[0, block, :] = dot((lower + upper).astype(BF), table_ref[0])
        spec_ref[1, block, :] = dot((lower - upper).astype(BF), table_ref[1])
        for i in (2 * half, 2 * half + 1):
            rows = slice(128 * i, 128 * i + 128)
            for parity in range(2):
                lanes = slice(MP * parity, MP * parity + MP)
                part_a, part_b = spec_ref[parity, rows, :MP], spec_ref[parity, rows, MP:]
                for k in range(NK):
                    g = NK * i + k
                    real = gain_ref[g : g + 1, lanes]
                    imag = gain_ref[12 + g : 13 + g, lanes]
                    out = slice(128 * k, 128 * k + 128)
                    filt_ref[i, parity, out, :MP] = (real * part_a + imag * part_b).astype(BF)
                    filt_ref[i, parity, out, MP:] = (real * part_b - imag * part_a).astype(BF)
            result = dot_nt(filt_ref[i, 0], places[0]) + sign * dot_nt(filt_ref[i, 1], places[1])
            result = (result * (2.0 / NLON)).astype(BF)
            held_ref[:, 256 * i + 192 : 256 * i + 256] = jnp.zeros((384, 64), BF)
            held_ref[:, 256 * i : 256 * i + 192] = result
    for k in range(NK):
        mixed = dot(filter_ref[k], held_ref[128 * k : 128 * k + 128, :]).astype(BF)
        for i in range(NR):
            part_ref[NK * i + k] = mixed[:, 256 * i : 256 * i + 192]
    copies = []
    totals = []
    for s in range(NZ):
        rows = slice(CB * s, CB * s + CB)
        parts = jnp.concatenate([part_ref[g, rows, :] for g in range(12)], axis=0)
        totals.append(dot(turned_ref[...], parts))
        spread_band(totals[s], 1, rows, base_ref, state_grad_ref)
        piece = pl.ds(CB * s, CB)
        copies.append(
            pltpu.make_async_copy(base_ref.at[piece], base_hbm.at[piece], sems.at[s])
        )
        copies[-1].start()
    for s in range(NZ):
        rows = slice(CB * s, CB * s + CB)
        spread_band(totals[s], 0, rows, first_ref, None)
        spread_band(totals[s], 2, rows, second_ref, None)
    for copy in copies:
        copy.wait()


def spread_band(total, band, rows, ref, added_ref):
    for first in range(2):
        base = 64 * band + CB * first
        lower, upper = total[base : base + CB], total[base + 32 : base + 32 + CB]
        middle = jnp.concatenate([lower[:, 128:], upper[:, 128:]], axis=1)
        for tile, value in enumerate((lower[:, :128], middle, upper[:, :128])):
            lanes = slice(384 * first + 128 * tile, 384 * first + 128 * tile + 128)
            if added_ref is not None:
                value = value + added_ref[rows, lanes]
            ref[rows, lanes] = value.astype(ref.dtype)


def sum_kernel(share, recv_ref, out_ref):
    rows, columns = out_ref.shape[0], recv_ref.shape[0]
    same = lax.rem(iota((rows, columns), 0), share) == lax.rem(iota((rows, columns), 1), share)
    out_ref[...] = dot(same.astype(F32).astype(BF), recv_ref[...]).astype(BF)


def field_kernel(base_hbm, first_ref, second_ref, grad_hbm, base_ref, grad_ref, sems):
    copies = bring([(base_hbm, base_ref)], sems)
    select = point_select()
    halo = first_ref[...].astype(F32) + second_ref[...].astype(F32)
    copies[0].wait()
    total = (base_ref[...] + halo).astype(BF)
    copies = []
    for n, (start, size) in enumerate(((0, 368), (368, 352))):
        rows = pl.ds(start, size)
        grad_ref[start : start + size, :] = dot_nt(select[start : start + size], total).astype(BF)
        copies.append(
            pltpu.make_async_copy(grad_ref.at[rows, :], grad_hbm.at[rows, :], sems.at[n])
        )
        copies[-1].start()
    for copy in copies:
        copy.wait()


def weights_kernel(scale, grads_ref, filter_ref, inner_ref, outer_ref):
    for s in range(NZ):
        for k in range(NK):
            base = 48 * s + CB * k
            filter_ref[k, CB * s : CB * s + CB, :] = grads_ref[base : base + CB, :].astype(F32) * scale
    outer_ref[...] = grads_ref[384:640, :].astype(F32) * scale
    inner_ref[:, :128] = grads_ref[640:768, :].astype(F32) * scale
    inner_ref[:, 128:] = grads_ref[768:896, :].astype(F32) * scale


def call(kernel, outs, flops, scratch=(), in_specs=None, out_specs=None):
    shapes = outs if isinstance(outs, tuple) else (outs,)
    moved = sum(math.prod(o.shape) * o.dtype.itemsize for o in shapes)
    if out_specs is None:
        out_specs = jax.tree.map(lambda _: pl.BlockSpec(memory_space=pltpu.VMEM), outs)
    return pl.pallas_call(
        kernel,
        out_shape=outs,
        in_specs=in_specs,
        out_specs=out_specs,
        scratch_shapes=scratch,
        compiler_params=pltpu.CompilerParams(vmem_limit_bytes=LIMIT),
        cost_estimate=pl.CostEstimate(flops=flops, bytes_accessed=2 * moved, transcendentals=0),
    )


def shaped(shape, dtype=BF):
    return jax.ShapeDtypeStruct(shape, dtype)


def in_hbm(shape, dtype=BF):
    return pltpu.HBM(shape, dtype)


def hold(value):
    return pltpu.with_memory_space_constraint(value, pltpu.HBM)


def vmem(count):
    return [pl.BlockSpec(memory_space=pltpu.VMEM)] * count


def hbm(count):
    return [pl.BlockSpec(memory_space=pltpu.HBM)] * count


def swapped(value, first):
    count = lax.axis_size("lat")
    pairs = []
    for low in range(first, count - 1, 2):
        pairs += [(low, low + 1), (low + 1, low)]
    return lax.ppermute(value, "lat", pairs)


def local(
    fields,
    cotangent,
    basis_weights,
    band_support,
    spectrum_real,
    spectrum_imag,
    filter_weights,
    inner_weights,
    outer_weights,
):
    group = lax.axis_size("ens") * lax.axis_size("lat")
    grad_scale = 1.0 / math.sqrt(group * NR * NLON)
    table = jnp.asarray(dft_table())

    field_points = fields[0].transpose(1, 0, 2).reshape(LON * NR, 128)
    cot_points = cotangent[0].transpose(1, 0, 2).reshape(LON * NR, 128)
    field_wide, send_fields = call(
        pack_kernel, (shaped((128, 768)), shaped((NZ, 32, 384))), 2 * 720 * 768 * 128,
        [pltpu.VMEM((720, 128), BF), pltpu.SemaphoreType.DMA((1,))], hbm(1)
    )(hold(field_points))
    own = lax.all_to_all(send_fields, "lon", 0, 0, tiled=True)

    cot_wide, coupling, turned, gains = call(
        prepare_kernel,
        (
            shaped((128, 768)),
            shaped((192, 192)),
            in_hbm((192, 192)),
            shaped((24, 2 * MP), F32),
        ),
        2 * 720 * 768 * 128,
        [
            pltpu.VMEM((192, 192), BF),
            pltpu.VMEM((720, 128), BF),
            pltpu.VMEM((NK, NR, 12), BF),
            pltpu.VMEM((NK, NR, MODES), F32),
            pltpu.VMEM((NK, NR, MODES), F32),
            pltpu.VMEM((1, 3), jnp.int32),
            pltpu.SemaphoreType.DMA((5,)),
        ],
        hbm(5),
        tuple(vmem(2) + hbm(1) + vmem(1)),
    )(
        hold(cot_points),
        hold(basis_weights),
        hold(spectrum_real),
        hold(spectrum_imag),
        hold(band_support),
    )

    first = swapped(own, 0)
    second = swapped(own, 1)
    work = [
        pltpu.VMEM((192, 2 * KP), BF),
        pltpu.VMEM((2, 192, 2 * MP), BF),
        pltpu.VMEM((2, KP, 2 * MP), BF),
        pltpu.SemaphoreType.DMA((3,)),
    ]
    send_filtered = call(
        filter_kernel, shaped((NZ, 96, 384)), 8 * 192 * KP * KP, work, vmem(5) + hbm(1)
    )(first, own, second, coupling, gains, hold(table))
    filtered = lax.all_to_all(send_filtered, "lon", 0, 0, tiled=True)

    back, grads, state_grad = call(
        mlp_kernel,
        (in_hbm((768, 128)), in_hbm((WIDE, 128)), in_hbm((128, 768), F32)),
        2 * 768 * 128 * 256 * 10,
        [
            pltpu.VMEM((768, 128), BF),
            pltpu.VMEM((WIDE, 128), BF),
            pltpu.VMEM((128, 768), F32),
            pltpu.SemaphoreType.DMA((3,)),
        ],
        vmem(6),
        tuple(hbm(3)),
    )(filtered, field_wide, cot_wide, filter_weights, inner_weights, outer_weights)
    back = lax.all_gather(back, "lon", tiled=True).reshape(NZ, 768, 128)

    share = WIDE // group

    def exchanged(value, axes):
        value = value.reshape(value.shape[0] // 2, 2, 128)
        return lax.all_to_all(value, axes, 0, 0, tiled=True).reshape(-1, 128)

    def summed(value, copies):
        return call(
            functools.partial(sum_kernel, share),
            shaped((copies * share, 128)),
            2 * copies * share * value.size,
            (),
            vmem(1),
        )(value)

    chunks = exchanged(grads, ("ens", "lat"))
    chunks = exchanged(summed(chunks, NZ), "lon")
    gathered = exchanged(summed(chunks, group), ("ens", "lat"))

    to_first, kept, to_second = call(
        adjoint_kernel,
        (shaped((128, 768)), in_hbm((128, 768), F32), shaped((128, 768))),
        4 * 512 * KP * KP + 4 * 1536 * KP * 192,
        [
            pltpu.VMEM((512, 2 * KP), BF),
            pltpu.VMEM((NZ, 256, 128), BF),
            pltpu.VMEM((2, 512, 2 * MP), F32),
            pltpu.VMEM((NR, 2, 384, 2 * MP), BF),
            pltpu.VMEM((384, 1024), BF),
            pltpu.VMEM((12, 128, 192), BF),
            pltpu.VMEM((192, 192), BF),
            pltpu.VMEM((128, 768), F32),
            pltpu.VMEM((128, 768), F32),
            pltpu.SemaphoreType.DMA((3 * NZ + 2,)),
        ],
        hbm(3) + vmem(3),
        tuple(vmem(1) + hbm(1) + vmem(1)),
    )(hold(back), hold(turned), hold(state_grad), gains, table, filter_weights)
    from_second = swapped(to_second, 1)
    from_first = swapped(to_first, 0)
    grad_points = call(
        field_kernel,
        in_hbm((LON * NR, 128)),
        2 * 720 * 768 * 128,
        [
            pltpu.VMEM((128, 768), F32),
            pltpu.VMEM((LON * NR, 128), BF),
            pltpu.SemaphoreType.DMA((2,)),
        ],
        hbm(1) + vmem(2),
        hbm(1)[0],
    )(hold(kept), from_second, from_first)

    filter_grad, inner_grad, outer_grad = call(
        functools.partial(weights_kernel, grad_scale),
        (shaped((NK, 128, 128), F32), shaped((128, 256), F32), shaped((256, 128), F32)),
        WIDE * 128,
        (),
        vmem(1),
    )(gathered)
    field_grad = grad_points.reshape(LON, NR, 128).transpose(1, 0, 2)[None]
    return (field_grad, filter_grad, inner_grad, outer_grad)


def solution(mesh):
    placed = (
        P("ens", "lat", "lon", None),
        P("ens", "lat", "lon", None),
        P(None, "lat", None),
        P("lat", None),
        P(None, "lat", None),
        P(None, "lat", None),
        P(),
        P(),
        P(),
    )
    return jax.shard_map(
        local,
        mesh=mesh,
        in_specs=placed,
        out_specs=(P("ens", "lat", "lon", None), P(), P(), P()),
        check_vma=False,
    )
```

```python
import functools
import math

import jax
import jax.numpy as jnp
import ml_dtypes
import numpy as np
from jax import lax
from jax.experimental import pallas as pl
from jax.experimental.pallas import tpu as pltpu
from jax.sharding import PartitionSpec as P

GELU_SCALE = 0.7978845608028654
CUBIC_TERM = 0.044715
BF = jnp.bfloat16
F32 = jnp.float32
NLON = 1440
NZ = 8
LON = 180
MODES = 720
MP = 384
KP = 768
CB = 16
NK = 3
NR = 4
WIDE = 896
LIMIT = 24 * 1024 * 1024


def dft_table():
    lane = np.arange(KP)
    tail = lane >= 512
    owner = np.where(tail, 2 * ((lane - 512) // 128) + (lane % 128 >= 64), lane // 128)
    place = np.where(tail, 128 + lane % 64, lane % 128)
    column = owner * LON + place
    tables = []
    for parity in range(2):
        frequency = 2 * np.arange(MP) + parity
        phase = 2.0 * math.pi * ((column[:, None] * frequency[None, :]) % NLON) / NLON
        valid = (place < LON)[:, None] & (frequency < MODES)[None, :]
        cos = np.where(valid, np.cos(phase), 0.0)
        sin = np.where(valid, -np.sin(phase), 0.0)
        tables.append(np.concatenate([cos, sin], axis=1))
    return np.stack(tables).astype(ml_dtypes.bfloat16)


def dot(a, b):
    return jnp.dot(a, b, preferred_element_type=F32)


def dot_tn(a, b):
    return lax.dot_general(a, b, (((0,), (0,)), ((), ())), preferred_element_type=F32)


def dot_nt(a, b):
    return lax.dot_general(a, b, (((1,), (1,)), ((), ())), preferred_element_type=F32)


def low_halves(a, b):
    return jnp.concatenate([a[:, :64], b[:, :64]], axis=1)


def high_halves(a, b):
    return jnp.concatenate([a[:, 64:], b[:, 64:]], axis=1)


def iota(shape, dim):
    return lax.broadcasted_iota(jnp.int32, shape, dim)


def point_select():
    lane = iota((8, 2 * 384), 1)
    first = (lane >= 384).astype(jnp.int32)
    lane = lane - 384 * first
    middle = (lane >= 128) & (lane < 256)
    upper = ((lane >= 192)).astype(jnp.int32)
    place = jnp.where(middle, 128 + (lane & 63), lane & 127)
    point = jnp.where(place < LON, place * NR + 2 * upper + first, -1)
    return (iota((LON * NR, 2 * 384), 0) == point[0:1]).astype(F32).astype(BF)


def tile_of(z):
    return 6 * (z // 4) + z % 4


def tile_of_pair(pair):
    return 6 * (pair // 2) + 4 + pair % 2


def unpack(ref, x_ref, base, rows):
    for z in range(NZ):
        lanes = slice(128 * tile_of(z), 128 * tile_of(z) + 128)
        x_ref[base : base + rows, lanes] = ref[z, :, 0:128]
        x_ref[base + rows : base + 2 * rows, lanes] = ref[z, :, 256:384]
    for pair in range(NZ // 2):
        lanes = slice(128 * tile_of_pair(pair), 128 * tile_of_pair(pair) + 128)
        even = ref[2 * pair, :, 128:256]
        odd = ref[2 * pair + 1, :, 128:256]
        x_ref[base : base + rows, lanes] = low_halves(even, odd)
        x_ref[base + rows : base + 2 * rows, lanes] = high_halves(even, odd)


def pack(ref, half, value, rows):
    for t in range(4):
        lanes = slice(128 * t, 128 * t + 128)
        ref[4 * half + t, :, 0:128] = value[:rows, lanes]
        ref[4 * half + t, :, 256:384] = value[rows:, lanes]
    for t in range(2):
        lanes = slice(512 + 128 * t, 640 + 128 * t)
        lower, upper = value[:rows, lanes], value[rows:, lanes]
        ref[4 * half + 2 * t, :, 128:256] = low_halves(lower, upper)
        ref[4 * half + 2 * t + 1, :, 128:256] = high_halves(lower, upper)


def bring(pairs, sems):
    copies = [
        pltpu.make_async_copy(source, target, sems.at[n]) for n, (source, target) in enumerate(pairs)
    ]
    for copy in copies:
        copy.start()
    return copies


def pack_kernel(points_hbm, wide_ref, send_ref, points_ref, sems):
    copies = bring([(points_hbm, points_ref)], sems)
    select = point_select()
    copies[0].wait()
    wide = dot_tn(points_ref[...], select).astype(BF)
    wide_ref[...] = wide
    for s in range(NZ):
        for first in range(2):
            send_ref[s, CB * first : CB * first + CB, :] = wide[
                CB * s : CB * s + CB, 384 * first : 384 * first + 384
            ]


def prepare_kernel(
    points_hbm,
    weights_hbm,
    real_hbm,
    imag_hbm,
    support_hbm,
    wide_ref,
    coupling_ref,
    turned_hbm,
    gain_ref,
    turned_ref,
    points_ref,
    weights_ref,
    real_ref,
    imag_ref,
    support_ref,
    sems,
):
    copies = bring(
        (
            (points_hbm, points_ref),
            (weights_hbm, weights_ref),
            (real_hbm, real_ref),
            (imag_hbm, imag_ref),
            (support_hbm, support_ref),
        ),
        sems,
    )
    select = point_select()
    copies[0].wait()
    wide_ref[...] = dot_tn(points_ref[...], select).astype(BF)

    for copy in copies[1:]:
        copy.wait()
    flip = lax.rem(lax.axis_index("lat"), 2) == 0
    lane = iota((1, 12), 1)
    seen = support_ref[...]
    seen = jnp.where(lane < 4, seen[:, 0:1], jnp.where(lane < 8, seen[:, 1:2], seen[:, 2:3]))
    seen = seen.astype(F32)
    rows = [weights_ref[k].astype(F32) for k in range(NK)]
    masked = jnp.concatenate([rows[k][i : i + 1] * seen for i in range(NR) for k in range(NK)], axis=0)
    turned = jnp.concatenate([masked[:, 8:12], masked[:, 4:8], masked[:, 0:4]], axis=1)
    masked = jnp.where(flip, turned, masked).astype(BF)
    size = 12 * CB
    expand = (iota((size, 12), 0) // CB == iota((size, 12), 1)).astype(F32).astype(BF)
    same = (iota((size, size), 0) & 15) == (iota((size, size), 1) & 15)
    wide = dot_nt(dot(expand, masked).astype(BF), expand)
    coupling_ref[...] = jnp.where(same, wide, 0.0).astype(BF)
    wide = dot_nt(dot_nt(expand, masked).astype(BF), expand)
    turned_ref[...] = jnp.where(same, wide, 0.0).astype(BF)
    copies = bring([(turned_ref, turned_hbm)], sems)

    lane = iota((MODES, 2 * MP), 1)
    odd = (lane >= MP).astype(jnp.int32)
    split = (iota((MODES, 2 * MP), 0) == 2 * (lane - MP * odd) + odd).astype(F32).astype(BF)
    first_half = jnp.where(iota((1, 2 * MP), 1) == 0, 0.5, 1.0).astype(F32)
    rest = []
    for ref in (real_ref, imag_ref):
        rows = [ref[k] for k in range(NK)]
        rest += [rows[k][i : i + 1] for i in range(NR) for k in range(NK)]
    rest = jnp.concatenate(rest, axis=0)
    pieces = []
    for step in range(3):
        piece = rest.astype(BF)
        rest = rest - piece.astype(F32)
        pieces.append(piece.astype(F32))
    moved = dot(jnp.concatenate(pieces, axis=0).astype(BF), split)
    gain_ref[...] = (moved[0:24] + moved[24:48] + moved[48:72]) * first_half
    copies[0].wait()


def spectral(value, parity, table_ref, gain_ref, filt_ref, sign):
    spec = dot(value, table_ref[parity])
    lanes = slice(MP * parity, MP * parity + MP)
    for g in range(12):
        rows = slice(CB * g, CB * g + CB)
        part_a, part_b = spec[rows, :MP], spec[rows, MP:]
        real = gain_ref[g : g + 1, lanes]
        imag = sign * gain_ref[12 + g : 13 + g, lanes]
        filt_ref[parity, rows, :MP] = (real * part_a - imag * part_b).astype(BF)
        filt_ref[parity, rows, MP:] = (real * part_b + imag * part_a).astype(BF)


def transform(lower, upper, table_ref, gain_ref, filt_ref, sign, copies):
    for parity, value in enumerate((lower + upper, lower - upper)):
        copies[parity].wait()
        spectral(value.astype(BF), parity, table_ref, gain_ref, filt_ref, sign)
    even = dot_nt(filt_ref[0], table_ref[0])
    odd = dot_nt(filt_ref[1], table_ref[1])
    scale = 2.0 / NLON
    return ((even + odd) * scale).astype(BF), ((even - odd) * scale).astype(BF)


def filter_kernel(
    first_ref,
    own_ref,
    second_ref,
    coupling_ref,
    gain_ref,
    table_hbm,
    send_ref,
    x_ref,
    filt_ref,
    table_ref,
    sems,
):
    copies = bring([(table_hbm.at[p], table_ref.at[p]) for p in range(2)], sems)
    for band, ref in enumerate((first_ref, own_ref, second_ref)):
        unpack(ref, x_ref, 64 * band, 32)
    coupling = coupling_ref[...]
    lower = dot(coupling, x_ref[:, :KP])
    upper = dot(coupling, x_ref[:, KP:])
    lower, upper = transform(lower, upper, table_ref, gain_ref, filt_ref, 1.0, copies)
    pack(send_ref, 0, lower, 96)
    pack(send_ref, 1, upper, 96)


def gelu_parts(hidden):
    inner_part = GELU_SCALE * (hidden + CUBIC_TERM * hidden * hidden * hidden)
    tangent = jnp.tanh(inner_part)
    gelu_value = 0.5 * hidden * (1.0 + tangent)
    gelu_slope = 0.5 * (1.0 + tangent) + 0.5 * hidden * (1.0 - tangent * tangent) * GELU_SCALE * (
        1.0 + 3.0 * CUBIC_TERM * hidden * hidden
    )
    return (gelu_value, gelu_slope)


def mlp_kernel(
    recv_ref,
    fields_ref,
    cot_ref,
    filter_ref,
    inner_ref,
    outer_ref,
    back_hbm,
    grads_ref,
    state_grad_hbm,
    back_ref,
    state_grad_ref,
    sems,
):
    mix = jnp.concatenate(
        [filter_ref[k, CB * s : CB * s + CB, :] for s in range(NZ) for k in range(NK)], axis=0
    )
    inner = inner_ref[...]
    outer = outer_ref[...]
    held = []
    for first in range(2):
        lanes = slice(384 * first, 384 * first + 384)
        filtered = jnp.concatenate(
            [recv_ref[s, 48 * first : 48 * first + 48, :] for s in range(NZ)], axis=0
        )
        cot = cot_ref[:, lanes]
        state = (fields_ref[:, lanes].astype(F32) + dot_tn(mix, filtered)).astype(BF)
        hidden = dot_tn(inner, state)
        value, slope = gelu_parts(hidden)
        active = value.astype(BF)
        d_hidden = (dot(outer, cot) * slope).astype(BF)
        d_state = cot.astype(F32) + dot(inner, d_hidden)
        state_grad_ref[:, lanes] = d_state
        d_state_b = d_state.astype(BF)
        for tile in range(3):
            base = 256 * tile + 128 * first
            back_ref[base : base + 128, :] = d_state_b[:, 128 * tile : 128 * tile + 128]
        held.append((filtered, d_state_b, active, cot, state, d_hidden))
    copies = bring(((back_ref, back_hbm), (state_grad_ref, state_grad_hbm)), sems)
    sums = None
    for filtered, d_state_b, active, cot, state, d_hidden in held:
        parts = (dot_nt(filtered, d_state_b), dot_nt(active, cot), dot_nt(state, d_hidden))
        sums = parts if sums is None else tuple(a + b for a, b in zip(sums, parts))
    grads_ref[0:384, :] = sums[0].astype(BF)
    grads_ref[384:640, :] = sums[1].astype(BF)
    grads_ref[640:768, :] = sums[2][:, :128].astype(BF)
    grads_ref[768:896, :] = sums[2][:, 128:].astype(BF)
    for copy in copies:
        copy.wait()


def adjoint_kernel(
    recv_hbm,
    turned_hbm,
    state_grad_hbm,
    gain_ref,
    table_ref,
    filter_ref,
    first_ref,
    base_hbm,
    second_ref,
    x_ref,
    middle_ref,
    spec_ref,
    filt_ref,
    held_ref,
    part_ref,
    turned_ref,
    state_grad_ref,
    base_ref,
    sems,
):
    pairs = [(recv_hbm.at[n, pl.ds(256, 256), :], middle_ref.at[n]) for n in range(NZ)]
    for half in range(2):
        for n in range(NZ):
            lanes = pl.ds(128 * tile_of(n), 128)
            rows = pl.ds(256 * half, 256)
            pairs.append((recv_hbm.at[n, pl.ds(512 * half, 256), :], x_ref.at[rows, lanes]))
    pairs += [(turned_hbm, turned_ref), (state_grad_hbm, state_grad_ref)]
    copies = bring(pairs, sems)
    z = lax.axis_index("lon")
    quarter = lax.rem(z, 4)
    sign = jnp.where(z < 4, 1.0, -1.0)
    main = pl.ds(pl.multiple_of(128 * quarter, 128), 128)
    tail = pl.ds(pl.multiple_of(512 + 64 * quarter, 64), 64)
    places = [
        jnp.concatenate([table_ref[p, main, :], table_ref[p, tail, :]], axis=0) for p in range(2)
    ]
    for half in range(2):
        for copy in copies[0 : 2 * NZ] if half == 0 else copies[2 * NZ :]:
            copy.wait()
        block = slice(256 * half, 256 * half + 256)
        for pair in range(NZ // 2):
            lanes = slice(128 * tile_of_pair(pair), 128 * tile_of_pair(pair) + 128)
            even, odd = middle_ref[2 * pair], middle_ref[2 * pair + 1]
            x_ref[block, lanes] = low_halves(even, odd) if half == 0 else high_halves(even, odd)
        lower = x_ref[block, :KP].astype(F32)
        upper = x_ref[block, KP:].astype(F32)
        spec_ref[0, block, :] = dot((lower + upper).astype(BF), table_ref[0])
        spec_ref[1, block, :] = dot((lower - upper).astype(BF), table_ref[1])
        for i in (2 * half, 2 * half + 1):
            rows = slice(128 * i, 128 * i + 128)
            for parity in range(2):
                lanes = slice(MP * parity, MP * parity + MP)
                part_a, part_b = spec_ref[parity, rows, :MP], spec_ref[parity, rows, MP:]
                for k in range(NK):
                    g = NK * i + k
                    real = gain_ref[g : g + 1, lanes]
                    imag = gain_ref[12 + g : 13 + g, lanes]
                    out = slice(128 * k, 128 * k + 128)
                    filt_ref[i, parity, out, :MP] = (real * part_a + imag * part_b).astype(BF)
                    filt_ref[i, parity, out, MP:] = (real * part_b - imag * part_a).astype(BF)
            result = dot_nt(filt_ref[i, 0], places[0]) + sign * dot_nt(filt_ref[i, 1], places[1])
            result = (result * (2.0 / NLON)).astype(BF)
            held_ref[:, 256 * i + 192 : 256 * i + 256] = jnp.zeros((384, 64), BF)
            held_ref[:, 256 * i : 256 * i + 192] = result
    for k in range(NK):
        mixed = dot(filter_ref[k], held_ref[128 * k : 128 * k + 128, :]).astype(BF)
        for i in range(NR):
            part_ref[NK * i + k] = mixed[:, 256 * i : 256 * i + 192]
    copies = []
    totals = []
    for s in range(NZ):
        rows = slice(CB * s, CB * s + CB)
        parts = jnp.concatenate([part_ref[g, rows, :] for g in range(12)], axis=0)
        totals.append(dot(turned_ref[...], parts))
        spread_band(totals[s], 1, rows, base_ref, state_grad_ref)
        piece = pl.ds(CB * s, CB)
        copies.append(
            pltpu.make_async_copy(base_ref.at[piece], base_hbm.at[piece], sems.at[s])
        )
        copies[-1].start()
    for s in range(NZ):
        rows = slice(CB * s, CB * s + CB)
        spread_band(totals[s], 0, rows, first_ref, None)
        spread_band(totals[s], 2, rows, second_ref, None)
    for copy in copies:
        copy.wait()


def spread_band(total, band, rows, ref, added_ref):
    for first in range(2):
        base = 64 * band + CB * first
        lower, upper = total[base : base + CB], total[base + 32 : base + 32 + CB]
        middle = jnp.concatenate([lower[:, 128:], upper[:, 128:]], axis=1)
        for tile, value in enumerate((lower[:, :128], middle, upper[:, :128])):
            lanes = slice(384 * first + 128 * tile, 384 * first + 128 * tile + 128)
            if added_ref is not None:
                value = value + added_ref[rows, lanes]
            ref[rows, lanes] = value.astype(ref.dtype)


def sum_kernel(share, recv_ref, out_ref):
    rows, columns = out_ref.shape[0], recv_ref.shape[0]
    same = lax.rem(iota((rows, columns), 0), share) == lax.rem(iota((rows, columns), 1), share)
    out_ref[...] = dot(same.astype(F32).astype(BF), recv_ref[...]).astype(BF)


def field_kernel(base_hbm, first_ref, second_ref, grad_hbm, base_ref, grad_ref, sems):
    copies = bring([(base_hbm, base_ref)], sems)
    select = point_select()
    halo = first_ref[...].astype(F32) + second_ref[...].astype(F32)
    copies[0].wait()
    total = (base_ref[...] + halo).astype(BF)
    copies = []
    for n, (start, size) in enumerate(((0, 368), (368, 352))):
        rows = pl.ds(start, size)
        grad_ref[start : start + size, :] = dot_nt(select[start : start + size], total).astype(BF)
        copies.append(
            pltpu.make_async_copy(grad_ref.at[rows, :], grad_hbm.at[rows, :], sems.at[n])
        )
        copies[-1].start()
    for copy in copies:
        copy.wait()


def weights_kernel(scale, grads_ref, filter_ref, inner_ref, outer_ref):
    for s in range(NZ):
        for k in range(NK):
            base = 48 * s + CB * k
            filter_ref[k, CB * s : CB * s + CB, :] = grads_ref[base : base + CB, :].astype(F32) * scale
    outer_ref[...] = grads_ref[384:640, :].astype(F32) * scale
    inner_ref[:, :128] = grads_ref[640:768, :].astype(F32) * scale
    inner_ref[:, 128:] = grads_ref[768:896, :].astype(F32) * scale


def call(kernel, outs, flops, scratch=(), in_specs=None, out_specs=None):
    shapes = outs if isinstance(outs, tuple) else (outs,)
    moved = sum(math.prod(o.shape) * o.dtype.itemsize for o in shapes)
    if out_specs is None:
        out_specs = jax.tree.map(lambda _: pl.BlockSpec(memory_space=pltpu.VMEM), outs)
    return pl.pallas_call(
        kernel,
        out_shape=outs,
        in_specs=in_specs,
        out_specs=out_specs,
        scratch_shapes=scratch,
        compiler_params=pltpu.CompilerParams(vmem_limit_bytes=LIMIT),
        cost_estimate=pl.CostEstimate(flops=flops, bytes_accessed=2 * moved, transcendentals=0),
    )


def shaped(shape, dtype=BF):
    return jax.ShapeDtypeStruct(shape, dtype)


def in_hbm(shape, dtype=BF):
    return pltpu.HBM(shape, dtype)


def hold(value):
    return pltpu.with_memory_space_constraint(value, pltpu.HBM)


def vmem(count):
    return [pl.BlockSpec(memory_space=pltpu.VMEM)] * count


def hbm(count):
    return [pl.BlockSpec(memory_space=pltpu.HBM)] * count


def swapped(value, first):
    count = lax.axis_size("lat")
    pairs = []
    for low in range(first, count - 1, 2):
        pairs += [(low, low + 1), (low + 1, low)]
    return lax.ppermute(value, "lat", pairs)


def local(
    fields,
    cotangent,
    basis_weights,
    band_support,
    spectrum_real,
    spectrum_imag,
    filter_weights,
    inner_weights,
    outer_weights,
):
    group = lax.axis_size("ens") * lax.axis_size("lat")
    grad_scale = 1.0 / math.sqrt(group * NR * NLON)
    table = jnp.asarray(dft_table())

    field_points = fields[0].transpose(1, 0, 2).reshape(LON * NR, 128)
    cot_points = cotangent[0].transpose(1, 0, 2).reshape(LON * NR, 128)
    field_wide, send_fields = call(
        pack_kernel, (shaped((128, 768)), shaped((NZ, 32, 384))), 2 * 720 * 768 * 128,
        [pltpu.VMEM((720, 128), BF), pltpu.SemaphoreType.DMA((1,))], hbm(1)
    )(hold(field_points))
    own = lax.all_to_all(send_fields, "lon", 0, 0, tiled=True)

    cot_wide, coupling, turned, gains = call(
        prepare_kernel,
        (
            shaped((128, 768)),
            shaped((192, 192)),
            in_hbm((192, 192)),
            shaped((24, 2 * MP), F32),
        ),
        2 * 720 * 768 * 128,
        [
            pltpu.VMEM((192, 192), BF),
            pltpu.VMEM((720, 128), BF),
            pltpu.VMEM((NK, NR, 12), BF),
            pltpu.VMEM((NK, NR, MODES), F32),
            pltpu.VMEM((NK, NR, MODES), F32),
            pltpu.VMEM((1, 3), jnp.int32),
            pltpu.SemaphoreType.DMA((5,)),
        ],
        hbm(5),
        tuple(vmem(2) + hbm(1) + vmem(1)),
    )(
        hold(cot_points),
        hold(basis_weights),
        hold(spectrum_real),
        hold(spectrum_imag),
        hold(band_support),
    )

    first = swapped(own, 0)
    second = swapped(own, 1)
    work = [
        pltpu.VMEM((192, 2 * KP), BF),
        pltpu.VMEM((2, 192, 2 * MP), BF),
        pltpu.VMEM((2, KP, 2 * MP), BF),
        pltpu.SemaphoreType.DMA((3,)),
    ]
    send_filtered = call(
        filter_kernel, shaped((NZ, 96, 384)), 8 * 192 * KP * KP, work, vmem(5) + hbm(1)
    )(first, own, second, coupling, gains, hold(table))
    filtered = lax.all_to_all(send_filtered, "lon", 0, 0, tiled=True)

    back, grads, state_grad = call(
        mlp_kernel,
        (in_hbm((768, 128)), shaped((WIDE, 128)), in_hbm((128, 768), F32)),
        2 * 768 * 128 * 256 * 10,
        [
            pltpu.VMEM((768, 128), BF),
            pltpu.VMEM((128, 768), F32),
            pltpu.SemaphoreType.DMA((2,)),
        ],
        vmem(6),
        tuple(hbm(1) + vmem(1) + hbm(1)),
    )(filtered, field_wide, cot_wide, filter_weights, inner_weights, outer_weights)
    back = lax.all_gather(back, "lon", tiled=True).reshape(NZ, 768, 128)

    share = WIDE // group

    def exchanged(value, axes):
        value = value.reshape(value.shape[0] // 2, 2, 128)
        return lax.all_to_all(value, axes, 0, 0, tiled=True).reshape(-1, 128)

    def summed(value, copies):
        return call(
            functools.partial(sum_kernel, share),
            shaped((copies * share, 128)),
            2 * copies * share * value.size,
            (),
            vmem(1),
        )(value)

    chunks = exchanged(grads, ("ens", "lat"))
    chunks = exchanged(summed(chunks, NZ), "lon")
    gathered = exchanged(summed(chunks, group), ("ens", "lat"))

    to_first, kept, to_second = call(
        adjoint_kernel,
        (shaped((128, 768)), in_hbm((128, 768), F32), shaped((128, 768))),
        4 * 512 * KP * KP + 4 * 1536 * KP * 192,
        [
            pltpu.VMEM((512, 2 * KP), BF),
            pltpu.VMEM((NZ, 256, 128), BF),
            pltpu.VMEM((2, 512, 2 * MP), F32),
            pltpu.VMEM((NR, 2, 384, 2 * MP), BF),
            pltpu.VMEM((384, 1024), BF),
            pltpu.VMEM((12, 128, 192), BF),
            pltpu.VMEM((192, 192), BF),
            pltpu.VMEM((128, 768), F32),
            pltpu.VMEM((128, 768), F32),
            pltpu.SemaphoreType.DMA((3 * NZ + 2,)),
        ],
        hbm(3) + vmem(3),
        tuple(vmem(1) + hbm(1) + vmem(1)),
    )(hold(back), hold(turned), hold(state_grad), gains, table, filter_weights)
    from_second = swapped(to_second, 1)
    from_first = swapped(to_first, 0)
    grad_points = call(
        field_kernel,
        in_hbm((LON * NR, 128)),
        2 * 720 * 768 * 128,
        [
            pltpu.VMEM((128, 768), F32),
            pltpu.VMEM((LON * NR, 128), BF),
            pltpu.SemaphoreType.DMA((2,)),
        ],
        hbm(1) + vmem(2),
        hbm(1)[0],
    )(hold(kept), from_second, from_first)

    filter_grad, inner_grad, outer_grad = call(
        functools.partial(weights_kernel, grad_scale),
        (shaped((NK, 128, 128), F32), shaped((128, 256), F32), shaped((256, 128), F32)),
        WIDE * 128,
        (),
        vmem(1),
    )(gathered)
    field_grad = grad_points.reshape(LON, NR, 128).transpose(1, 0, 2)[None]
    return (field_grad, filter_grad, inner_grad, outer_grad)


def solution(mesh):
    placed = (
        P("ens", "lat", "lon", None),
        P("ens", "lat", "lon", None),
        P(None, "lat", None),
        P("lat", None),
        P(None, "lat", None),
        P(None, "lat", None),
        P(),
        P(),
        P(),
    )
    return jax.shard_map(
        local,
        mesh=mesh,
        in_specs=placed,
        out_specs=(P("ens", "lat", "lon", None), P(), P(), P()),
        check_vma=False,
    )
```
